128 devices in a mesh: row: 8 (over z_lo, x), col: 16 (over z_hi, y, core).
Axes of the slice: x: 4, y: 4, z: 4 (z_hi: 2, z_lo: 2; z = z_hi * 2 + z_lo), core: 2. Of those that a mesh axis runs over, the one named last changes fastest.
Arguments:
- inputs: bfloat16 [512, 8192], P(('row', 'col')), may hold values from -36 to 36
- rms_gain_vector: float32 [8192], replicated, may hold values from 0.1 to 1.9
- gate_weight: bfloat16 [8192, 28672], P('row', 'col'), may hold values from -0.0625 to 0.0625
- up_weight: bfloat16 [8192, 28672], P('row', 'col'), may hold values from -0.0625 to 0.0625
- down_weight: bfloat16 [28672, 8192], P('col', 'row'), may hold values from -0.03125 to 0.03125
- out_grad: bfloat16 [512, 8192], P(('row', 'col')), may hold values from -6 to 6
Outputs:
- outputs: bfloat16 [512, 8192], P(('row', 'col'))
- input_gradient: bfloat16 [512, 8192], P(('row', 'col'))
- norm_gain_gradient: float32 [8192], replicated
- gate_weight_grad: bfloat16 [8192, 28672], P('row', 'col')
- up_weight_grad: bfloat16 [8192, 28672], P('row', 'col')
- down_weight_grad: bfloat16 [28672, 8192], P('col', 'row')
The draws below stay inside these ranges and needn't reach their ends.
All inputs are finite; a program needn't handle non-finite values.
Results may differ from the reference program's by a relative error of at most 0.0067.
Values may be sent and summed in bfloat16 or wider, within the bound.
No kernel may reach another device: no remote copies, remote signals or barrier semaphores. Data moves between devices by JAX's collectives and lax.ppermute only.
A program may use at most 128 MiB of HBM per device.

```python
import math
import jax
import jax.numpy as jnp
from jax import lax

D = 8192
FF = 28672
TOKENS = 512


def draw_inputs(key, part):
    key = jax.random.fold_in(key, 11)
    key_rows, key_cols, key_base = jax.random.split(key, 3)
    row_scale = 0.3 * jnp.exp(jax.random.uniform(key_rows, (TOKENS, 1), jnp.float32, 0.0, math.log(10.0)))
    col_scale = 0.3 * jnp.exp(jax.random.uniform(key_cols, (1, D), jnp.float32, 0.0, math.log(10.0)))
    base = jax.random.normal(key_base, (TOKENS, D), jnp.float32)
    base = jnp.clip(base, -4.0, 4.0)
    return (base * row_scale * col_scale).astype(jnp.bfloat16)


def steps_of(stream_key, dims, cuts, smallest, largest):
    gain, own = 1.0, jax.random.fold_in(stream_key, 6)
    for dim, blocks in cuts:
        heights = jnp.exp(jax.random.uniform(jax.random.fold_in(own, dim), (blocks,), jnp.float32, smallest / len(cuts), largest / len(cuts)))
        gain = gain * jnp.repeat(heights, dims[dim] // blocks).reshape([-1 if axis == dim else 1 for axis in range(len(dims))])
    return gain


def centred(key, dims, width, most, pieces=(), dtype=jnp.bfloat16):
    array = width * jax.random.normal(key, dims, jnp.float32)
    if pieces:
        array = array * steps_of(key, dims, pieces, -0.22, 0.18)
    return jnp.clip(array, -most, most).astype(dtype)


def setup_inputs(seed: int = 0) -> dict:
    seeds = jax.random.split(jax.random.key(seed), 7)
    inputs = draw_inputs(jax.random.fold_in(seeds[6], 71), 0)
    rms_gain_vector = jnp.clip(1.0 + 0.18 * jax.random.normal(seeds[1], (D,), jnp.float32), 0.1, 1.9)
    gate_weight = centred(seeds[2], (D, FF), D ** -0.5, 0.0625, ((0, 8), (1, 16)))
    up_weight = centred(seeds[3], (D, FF), D ** -0.5, 0.0625, ((0, 8), (1, 16)))
    down_weight = centred(seeds[4], (FF, D), FF ** -0.5, 0.03125, ((0, 16), (1, 8)))
    out_grad = centred(seeds[5], (TOKENS, D), 1.0, 6.0, ((0, 128),))
    return dict(inputs=inputs, rms_gain_vector=rms_gain_vector, gate_weight=gate_weight, up_weight=up_weight, down_weight=down_weight, out_grad=out_grad)


EPS = 1e-05

def reference(inputs, rms_gain_vector, gate_weight, up_weight, down_weight, out_grad):
    value_entries = inputs.astype(jnp.float32)
    inverse_root_mean_square = lax.rsqrt(lax.optimization_barrier(jnp.mean(value_entries * value_entries, axis=1, keepdims=True)) + EPS)
    normalized_estimate = value_entries * inverse_root_mean_square
    normalized_input = (normalized_estimate * rms_gain_vector).astype(jnp.bfloat16)
    gate = jnp.dot(normalized_input, gate_weight, preferred_element_type=jnp.float32)
    up = jnp.dot(normalized_input, up_weight, preferred_element_type=jnp.float32)
    hidden = (jax.nn.silu(gate) * up).astype(jnp.bfloat16)
    outputs = jnp.dot(hidden, down_weight, preferred_element_type=jnp.float32).astype(jnp.bfloat16)
    down_weight_grad = jnp.dot(hidden.T, out_grad, preferred_element_type=jnp.float32).astype(jnp.bfloat16)
    hidden_grad = jnp.dot(out_grad, down_weight.T, preferred_element_type=jnp.float32)
    sigma = jax.nn.sigmoid(gate)
    gate_grad = (hidden_grad * up * sigma * (1.0 + gate * (1.0 - sigma))).astype(jnp.bfloat16)
    up_grad = (hidden_grad * jax.nn.silu(gate)).astype(jnp.bfloat16)
    gate_weight_grad = jnp.dot(normalized_input.T, gate_grad, preferred_element_type=jnp.float32).astype(jnp.bfloat16)
    up_weight_grad = jnp.dot(normalized_input.T, up_grad, preferred_element_type=jnp.float32).astype(jnp.bfloat16)
    normalized_gradient = jnp.dot(gate_grad, gate_weight.T, preferred_element_type=jnp.float32)
    normalized_gradient = normalized_gradient + jnp.dot(up_grad, up_weight.T, preferred_element_type=jnp.float32)
    norm_gain_gradient = lax.optimization_barrier(jnp.sum(normalized_gradient * normalized_estimate, axis=0))
    gain_scaled_input = normalized_gradient * rms_gain_vector
    input_gradient = inverse_root_mean_square * (gain_scaled_input - normalized_estimate * lax.optimization_barrier(jnp.mean(gain_scaled_input * normalized_estimate, axis=1, keepdims=True)))
    return (outputs, input_gradient.astype(jnp.bfloat16), norm_gain_gradient, gate_weight_grad, up_weight_grad, down_weight_grad)
```

```python
import jax
import jax.numpy as jnp
from jax import lax
from jax.sharding import PartitionSpec as P

EPS = 1e-05
F32 = jnp.float32
BF16 = jnp.bfloat16
ZS, XS, HS, YS, CS = 2, 4, 2, 4, 2


def row_shift(dz, dx):
    return [
        (z * XS + x, (z + dz) % ZS * XS + (x + dx) % XS)
        for z in range(ZS)
        for x in range(XS)
    ]


def col_shift(dh, dy, dc):
    return [
        ((h * YS + y) * CS + c, ((h + dh) % HS * YS + (y + dy) % YS) * CS + (c + dc) % CS)
        for h in range(HS)
        for y in range(YS)
        for c in range(CS)
    ]


def to_row(value, dz, dx):
    return lax.ppermute(value, "row", row_shift(dz, dx))


def to_col(value, dh, dy, dc):
    return lax.ppermute(value, "col", col_shift(dh, dy, dc))


def product(left, right):
    return jnp.dot(left, right, preferred_element_type=F32)


def product_right_t(left, right):
    return lax.dot_general(left, right, (((1,), (1,)), ((), ())), preferred_element_type=F32)


def product_left_t(left, right):
    return lax.dot_general(left, right, (((0,), (0,)), ((), ())), preferred_element_type=F32)


def rounded(value):
    return lax.reduce_precision(value, 8, 7)


def parts_of(value, count):
    parts = []
    for _ in range(count):
        top = rounded(value)
        parts.append(top.astype(BF16))
        value = value - top
    return parts


def gather_tokens(block, x, z):
    n = block.shape[1]
    both = {0: block, 1: to_col(block, 1, 0, 0)}
    pair = jnp.concatenate([both[0], both[1]], axis=0)
    got = {0: pair}
    for dy in (1, 3, 2):
        got[(-dy) % YS] = to_col(pair, 0, dy, 0)
    own = jnp.zeros((256, n), BF16)
    for dy in range(YS):
        for dh in range(HS):
            slot = (dh * 2 + dy // 2 - x) % XS
            own = lax.dynamic_update_slice(
                own, got[dy][dh * 32 : dh * 32 + 32], (slot * 64 + dy % 2 * 32, 0)
            )
    other = to_col(own, 0, 0, 1)
    full = jnp.zeros((512, n), BF16)
    full = lax.dynamic_update_slice(full, own, (z * 256, 0))
    return lax.dynamic_update_slice(full, other, ((1 - z) * 256, 0))


def sum_over_row(near, far):
    m12 = to_row(far[2].astype(BF16), 1, 0).astype(F32)
    m11 = to_row(far[1].astype(BF16), 0, 1).astype(F32)
    m13 = to_row(far[3].astype(BF16), 0, 3).astype(F32)
    a02 = near[2] + m12
    h = a02.shape[0] // 2
    n1 = to_row(a02[:h].astype(BF16), 0, 1).astype(F32)
    n2 = to_row(a02[h:].astype(BF16), 0, 3).astype(F32)
    q = to_row((far[0] + m11 + m13).astype(BF16), 1, 0).astype(F32)
    a01 = jnp.concatenate([near[1][:h] + n1, near[1][h:]], axis=0)
    a03 = jnp.concatenate([near[3][:h], near[3][h:] + n2], axis=0)
    r1 = to_row(a01.astype(BF16), 0, 1).astype(F32)
    r2 = to_row(a03.astype(BF16), 0, 3).astype(F32)
    return near[0] + q + r1 + r2


def gather_over_row(own):
    h = own.shape[0] // 2
    a = to_row(own, 0, 1)
    b = to_row(own, 0, 3)
    p = to_row(own, 1, 0)
    a2 = to_row(a[:h], 0, 1)
    b2 = to_row(b[h:], 0, 3)
    pa = to_row(p, 0, 1)
    pb = to_row(p, 0, 3)
    across = jnp.concatenate([a2, b2], axis=0)
    p2 = to_row(across, 1, 0)
    return jnp.concatenate([own, b, across, a, p, pb, p2, pa], axis=0)


def sum_over_col(partial, gain_partial, x, z):
    keep = lax.dynamic_slice(partial, (z * 256, 0), (256, 2048))
    give = lax.dynamic_slice(partial, ((1 - z) * 256, 0), (256, 2048))
    give = jnp.concatenate([give, jnp.pad(gain_partial, ((0, 0), (0, 2048 - 128)))], axis=0)
    taken = to_col(give, 0, 0, 1)
    keep = keep + taken[:256]
    gain_partial = gain_partial + taken[256:, :128]
    gain_parts = jnp.concatenate(parts_of(gain_partial, 2) + [jnp.zeros((16, 128), BF16)], axis=0)

    def piece(dh, dy):
        slot = (dh * 2 + dy // 2 - x) % XS
        return lax.dynamic_slice(keep, (slot * 64 + dy % 2 * 32, 0), (32, 2048))

    def gain_of(parts):
        return parts[:8].astype(F32) + parts[8:16].astype(F32)

    total = piece(0, 0)
    gains = {(0, 0): gain_of(gain_parts)}
    for dh, dy in ((0, 1), (0, 3), (1, 0), (0, 2), (1, 1), (1, 3), (1, 2)):
        message = jnp.concatenate([piece(dh, dy).astype(BF16), gain_parts], axis=1)
        got = to_col(message, dh, dy, 0)
        total = total + got[:, :2048].astype(F32)
        gains[dh, dy] = gain_of(got[:, 2048:])
    over_y = [
        (gains[dh, 0] + gains[dh, 2]) + (gains[dh, 1] + gains[dh, 3]) for dh in range(HS)
    ]
    return total, over_y[0] + over_y[1]


def per_device(inputs, rms_gain_vector, gate_weight, up_weight, down_weight, out_grad):
    row = lax.axis_index("row")
    z, x = row // XS, row % XS
    width = gate_weight.shape[1]

    value_entries = inputs.astype(F32)
    inverse_rms = lax.rsqrt(jnp.mean(value_entries * value_entries, axis=1, keepdims=True) + EPS)
    side = jnp.concatenate(parts_of(inverse_rms, 3) + [jnp.zeros((4, 125), BF16)], axis=1)
    message = jnp.concatenate(
        [
            inputs.reshape(4, 8, 1024),
            out_grad.reshape(4, 8, 1024),
            jnp.broadcast_to(side[:, None, :], (4, 8, 128)),
        ],
        axis=2,
    )
    block = lax.all_to_all(message, "row", split_axis=1, concat_axis=0, tiled=True)
    tokens = gather_tokens(block.reshape(32, 2176), x, z)

    inverse_full = (
        tokens[:, 2048:2049].astype(F32)
        + tokens[:, 2049:2050].astype(F32)
        + tokens[:, 2050:2051].astype(F32)
    )
    gain_block = lax.dynamic_slice(rms_gain_vector, (row * 1024,), (1024,))
    estimate = tokens[:, :1024].astype(F32) * inverse_full
    normed = (estimate * gain_block).astype(BF16)
    grad_full = tokens[:, 1024:2048]

    def partials(rows):
        return jnp.concatenate(
            [
                product(normed[rows], gate_weight),
                product(normed[rows], up_weight),
                product_right_t(grad_full[rows], down_weight),
            ],
            axis=1,
        )

    far = partials(slice(256, 512)).reshape(4, 64, 3 * width)
    near = partials(slice(0, 256)).reshape(4, 64, 3 * width)
    sums = sum_over_row(near, far)
    gate, up, hidden_grad = sums[:, :width], sums[:, width : 2 * width], sums[:, 2 * width :]
    sigma = jax.nn.sigmoid(gate)
    silu = gate * sigma
    units = jnp.concatenate(
        [
            (silu * up).astype(BF16),
            (hidden_grad * up * sigma * (1.0 + gate * (1.0 - sigma))).astype(BF16),
            (hidden_grad * silu).astype(BF16),
        ],
        axis=1,
    )
    units = gather_over_row(units)
    hidden, gate_grad, up_grad = units[:, :width], units[:, width : 2 * width], units[:, 2 * width :]

    partial_out = product(hidden, down_weight)
    partial_grad = product_right_t(gate_grad, gate_weight) + product_right_t(up_grad, up_weight)
    gain_partial = jnp.sum(partial_grad * estimate, axis=0).reshape(8, 128)
    total, gain_total = sum_over_col(
        jnp.concatenate([partial_out, partial_grad], axis=1), gain_partial, x, z
    )
    down_weight_grad = product_left_t(hidden, grad_full).astype(BF16)
    gate_weight_grad = product_left_t(normed, gate_grad).astype(BF16)
    up_weight_grad = product_left_t(normed, up_grad).astype(BF16)

    grad_parts = parts_of(total[:, 1024:], 2)
    gain_parts = jnp.concatenate([p.reshape(4, 256) for p in parts_of(gain_total, 2)], axis=1)
    message = jnp.concatenate(
        [
            total[:, :1024].astype(BF16).reshape(8, 4, 1024),
            grad_parts[0].reshape(8, 4, 1024),
            grad_parts[1].reshape(8, 4, 1024),
            jnp.broadcast_to(gain_parts[None], (8, 4, 512)),
        ],
        axis=2,
    )
    back = lax.all_to_all(message, "row", split_axis=0, concat_axis=0, tiled=True)
    outputs = jnp.transpose(back[:, :, :1024], (1, 0, 2)).reshape(4, 8192)
    normed_grad = back[:, :, 1024:2048].astype(F32) + back[:, :, 2048:3072].astype(F32)
    normed_grad = jnp.transpose(normed_grad, (1, 0, 2)).reshape(4, 8192)
    gain_grad = back[:, :, 3072:3328].astype(F32) + back[:, :, 3328:].astype(F32)

    normalized = value_entries * inverse_rms
    scaled = normed_grad * rms_gain_vector
    input_gradient = inverse_rms * (
        scaled - normalized * jnp.mean(scaled * normalized, axis=1, keepdims=True)
    )
    return (
        outputs,
        input_gradient.astype(BF16),
        gain_grad.reshape(8192),
        gate_weight_grad,
        up_weight_grad,
        down_weight_grad,
    )


def solution(mesh):
    in_specs = (
        P(("row", "col"), None),
        P(),
        P("row", "col"),
        P("row", "col"),
        P("col", "row"),
        P(("row", "col"), None),
    )
    out_specs = (
        P(("row", "col"), None),
        P(("row", "col"), None),
        P(),
        P("row", "col"),
        P("row", "col"),
        P("col", "row"),
    )
    return jax.shard_map(
        per_device, mesh=mesh, in_specs=in_specs, out_specs=out_specs, check_vma=False
    )
```

```python
import jax
import jax.numpy as jnp
from jax import lax
from jax.sharding import PartitionSpec as P

EPS = 1e-05
F32 = jnp.float32
BF16 = jnp.bfloat16
ZS, XS, HS, YS, CS = 2, 4, 2, 4, 2


def send(value, z=0, x=0, h=0, y=0, c=0):
    pairs = []
    for z0 in range(ZS):
        for x0 in range(XS):
            for h0 in range(HS):
                for y0 in range(YS):
                    for c0 in range(CS):
                        source = (((z0 * XS + x0) * HS + h0) * YS + y0) * CS + c0
                        z1, x1, h1 = (z0 + z) % ZS, (x0 + x) % XS, (h0 + h) % HS
                        y1, c1 = (y0 + y) % YS, (c0 + c) % CS
                        pairs.append((source, (((z1 * XS + x1) * HS + h1) * YS + y1) * CS + c1))
    return lax.ppermute(value, ("row", "col"), pairs)


def product(left, right):
    return jnp.dot(left, right, preferred_element_type=F32)


def product_right_t(left, right):
    return lax.dot_general(left, right, (((1,), (1,)), ((), ())), preferred_element_type=F32)


def product_left_t(left, right):
    return lax.dot_general(left, right, (((0,), (0,)), ((), ())), preferred_element_type=F32)


def rounded(value):
    return lax.reduce_precision(value, 8, 7)


def parts_of(value, count):
    parts = []
    for _ in range(count):
        top = rounded(value)
        parts.append(top.astype(BF16))
        value = value - top
    return parts


def gather_tokens(inputs, inverse_rms, out_grad, z, x):
    side = jnp.concatenate(parts_of(inverse_rms, 3) + [jnp.zeros((4, 125), BF16)], axis=1)
    halves = [
        jnp.concatenate(
            [inputs[:, i * 4096 : i * 4096 + 4096], out_grad[:, i * 4096 : i * 4096 + 4096], side],
            axis=1,
        )
        for i in range(ZS)
    ]
    same = jnp.where(z == 0, halves[0], halves[1])
    cross = jnp.where(z == 0, halves[1], halves[0])
    got = [
        [same, send(same, h=1)],
        [send(cross, z=1), send(cross, z=1, h=1)],
    ]
    rows = jnp.concatenate([got[0][0], got[0][1], got[1][0], got[1][1]], axis=0)
    blocks = jnp.stack(
        [
            jnp.concatenate(
                [
                    rows[:, i * 1024 : i * 1024 + 1024],
                    rows[:, 4096 + i * 1024 : 5120 + i * 1024],
                    rows[:, 8192:],
                ],
                axis=1,
            )
            for i in range(XS)
        ]
    )

    def block_for(dx):
        return lax.dynamic_index_in_dim(blocks, (x + dx) % XS, 0, keepdims=False)

    over_x = {0: block_for(0)}
    for dx in (1, 3, 2):
        over_x[-dx % XS] = send(block_for(dx), x=dx)
    own = jnp.concatenate([over_x[i][s : s + 8] for s in (0, 8) for i in range(XS)], axis=0)
    over_y = {0: own}
    for dy in (1, 3, 2):
        over_y[-dy % YS] = send(own, y=dy)
    core = jnp.stack([over_y[i].reshape(8, 8, -1) for i in range(YS)], axis=1)
    core = core.reshape(256, -1)
    other = send(core, c=1)
    both = jnp.stack([core.reshape(8, 32, -1), other.reshape(8, 32, -1)], axis=1)
    return both.reshape(512, -1)


def sum_over_row(near, far):
    m12 = send(far[2].astype(BF16), z=1).astype(F32)
    m11 = send(far[1].astype(BF16), x=1).astype(F32)
    m13 = send(far[3].astype(BF16), x=3).astype(F32)
    a02 = near[2] + m12
    h = a02.shape[0] // 2
    n1 = send(a02[:h].astype(BF16), x=1).astype(F32)
    n2 = send(a02[h:].astype(BF16), x=3).astype(F32)
    q = send((far[0] + m11 + m13).astype(BF16), z=1).astype(F32)
    a01 = jnp.concatenate([near[1][:h] + n1, near[1][h:]], axis=0)
    a03 = jnp.concatenate([near[3][:h], near[3][h:] + n2], axis=0)
    r1 = send(a01.astype(BF16), x=1).astype(F32)
    r2 = send(a03.astype(BF16), x=3).astype(F32)
    return near[0] + q + r1 + r2


def gather_over_row(own):
    h = own.shape[0] // 2
    a = send(own, x=1)
    b = send(own, x=3)
    p = send(own, z=1)
    a2 = send(a[:h], x=1)
    b2 = send(b[h:], x=3)
    pa = send(p, x=1)
    pb = send(p, x=3)
    across = jnp.concatenate([a2, b2], axis=0)
    p2 = send(across, z=1)
    return (
        jnp.concatenate([own, b, across, a], axis=0),
        jnp.concatenate([p, pb, p2, pa], axis=0),
    )


def sum_to_owners(partial, gain_partial):
    side = jnp.pad(gain_partial, ((0, 248), (0, 0)))
    split = partial.reshape(8, 2, 32, 2048)
    message = jnp.concatenate([split[:, 1].reshape(256, 2048), side], axis=1)
    taken = send(message, c=1)
    keep = split[:, 0].reshape(256, 2048) + taken[:, :2048]
    gain = gain_partial + taken[:8, 2048:]
    gain_parts = jnp.concatenate(parts_of(gain, 2) + [jnp.zeros((48, 128), BF16)], axis=0)

    def gain_of(parts):
        return parts[:8].astype(F32) + parts[8:16].astype(F32)

    over_y = keep.reshape(8, 4, 8, 2048)
    total = over_y[:, 0].reshape(64, 2048)
    gains = {0: gain_of(gain_parts)}
    for dy in (1, 3, 2):
        message = over_y[:, dy].reshape(64, 2048).astype(BF16)
        got = send(jnp.concatenate([message, gain_parts], axis=1), y=dy)
        total = total + got[:, :2048].astype(F32)
        gains[dy] = gain_of(got[:, 2048:])
    gain = (gains[0] + gains[2]) + (gains[1] + gains[3])

    over_z = total.reshape(2, 4, 2, 4, 2048)
    side = jnp.pad(gain, ((0, 8), (0, 0)))

    def message_for(dz, dh):
        return jnp.concatenate([over_z[dz, :, dh].reshape(16, 2048), side], axis=1)

    sums = []
    for dz in range(ZS):
        mine = message_for(dz, 0)
        if dz:
            mine = send(mine, z=dz)
        sums.append(mine + send(message_for(dz, 1), z=dz, h=1))

    def last(total):
        grad = parts_of(total[:, 1024:2048], 2)
        return jnp.concatenate([total[:, :1024].astype(BF16), grad[0], grad[1]], axis=1)

    def gain_rows(total):
        return jnp.concatenate([p.reshape(4, 256) for p in parts_of(total[:8, 2048:], 2)], axis=1)

    ready = [last(total).reshape(4, 4, 3072) for total in sums]
    gains = [gain_rows(total) for total in sums]
    result = {}
    for dx in (0, 1, 3, 2):
        message = jnp.concatenate(
            [jnp.concatenate([ready[dz][dx], gains[dz]], axis=1) for dz in range(ZS)], axis=0
        )
        got = send(message, x=dx) if dx else message
        for dz in range(ZS):
            part = got[dz * 4 : dz * 4 + 4]
            result[dz, -dx % XS] = (
                part[:, :1024],
                part[:, 1024:2048].astype(F32) + part[:, 2048:3072].astype(F32),
                part[:, 3072:3328].astype(F32) + part[:, 3328:].astype(F32),
            )
    return result


def in_order(pieces, z, x):
    first = pieces[0, 0]
    stacked = jnp.zeros((8,) + first.shape, first.dtype)
    for (dz, dx), piece in pieces.items():
        place = (z + dz) % ZS * XS + (x + dx) % XS
        stacked = lax.dynamic_update_slice(stacked, piece[None], (place, 0, 0))
    return stacked


def per_device(inputs, rms_gain_vector, gate_weight, up_weight, down_weight, out_grad):
    row = lax.axis_index("row")
    z, x = row // XS, row % XS
    width = gate_weight.shape[1]

    value_entries = inputs.astype(F32)
    inverse_rms = lax.rsqrt(jnp.mean(value_entries * value_entries, axis=1, keepdims=True) + EPS)
    tokens = gather_tokens(inputs, inverse_rms, out_grad, z, x)
    inverse_full = (
        tokens[:, 2048:2049].astype(F32)
        + tokens[:, 2049:2050].astype(F32)
        + tokens[:, 2050:2051].astype(F32)
    )
    gain_block = lax.dynamic_slice(rms_gain_vector, (row * 1024,), (1024,))
    estimate = tokens[:, :1024].astype(F32) * inverse_full
    normed = (estimate * gain_block).astype(BF16)
    grad_full = tokens[:, 1024:2048]

    def partials(normed, grad):
        return jnp.concatenate(
            [
                product(normed, gate_weight),
                product(normed, up_weight),
                product_right_t(grad, down_weight),
            ],
            axis=1,
        ).reshape(4, 64, 3 * width)

    far = partials(normed[256:], grad_full[256:])
    near = partials(normed[:256], grad_full[:256])
    sums = sum_over_row(near, far)
    gate, up, hidden_grad = sums[:, :width], sums[:, width : 2 * width], sums[:, 2 * width :]
    sigma = jax.nn.sigmoid(gate)
    silu = gate * sigma
    units = jnp.concatenate(
        [
            (silu * up).astype(BF16),
            (hidden_grad * up * sigma * (1.0 + gate * (1.0 - sigma))).astype(BF16),
            (hidden_grad * silu).astype(BF16),
        ],
        axis=1,
    )
    units = gather_over_row(units)

    def back(units):
        hidden, gate_grad, up_grad = units[:, :width], units[:, width : 2 * width], units[:, 2 * width :]
        grad = product_right_t(gate_grad, gate_weight) + product_right_t(up_grad, up_weight)
        return jnp.concatenate([product(hidden, down_weight), grad], axis=1)

    partial = jnp.concatenate([back(units[0]), back(units[1])], axis=0)
    gain_partial = jnp.sum(partial[:, 1024:] * estimate, axis=0).reshape(8, 128)
    result = sum_to_owners(partial, gain_partial)

    units = jnp.concatenate(units, axis=0)
    hidden, gate_grad, up_grad = units[:, :width], units[:, width : 2 * width], units[:, 2 * width :]
    down_weight_grad = product_left_t(hidden, grad_full).astype(BF16)
    gate_weight_grad = product_left_t(normed, gate_grad).astype(BF16)
    up_weight_grad = product_left_t(normed, up_grad).astype(BF16)

    def tokens_of(index):
        stacked = in_order({k: v[index] for k, v in result.items()}, z, x)
        return jnp.transpose(stacked, (1, 0, 2)).reshape(4, 8192)

    outputs = tokens_of(0)
    normed_grad = tokens_of(1)
    gain_grad = in_order({k: v[2] for k, v in result.items()}, z, x).reshape(8192)

    normalized = value_entries * inverse_rms
    scaled = normed_grad * rms_gain_vector
    input_gradient = inverse_rms * (
        scaled - normalized * jnp.mean(scaled * normalized, axis=1, keepdims=True)
    )
    return (
        outputs,
        input_gradient.astype(BF16),
        gain_grad,
        gate_weight_grad,
        up_weight_grad,
        down_weight_grad,
    )


def solution(mesh):
    in_specs = (
        P(("row", "col"), None),
        P(),
        P("row", "col"),
        P("row", "col"),
        P("col", "row"),
        P(("row", "col"), None),
    )
    out_specs = (
        P(("row", "col"), None),
        P(("row", "col"), None),
        P(),
        P("row", "col"),
        P("row", "col"),
        P("col", "row"),
    )
    return jax.shard_map(
        per_device, mesh=mesh, in_specs=in_specs, out_specs=out_specs, check_vma=False
    )
```

```python
import jax
import jax.numpy as jnp
from jax import lax
from jax.sharding import Mesh, PartitionSpec as P

EPS = 1e-05
F32 = jnp.float32
BF16 = jnp.bfloat16
ZS, XS, HS, YS, CS = 2, 4, 2, 4, 2
AXES = ("z", "x", "h", "y", "core")


def send(value, z=0, x=0, h=0, y=0, c=0):
    pairs = []
    for z0 in range(ZS):
        for x0 in range(XS):
            for h0 in range(HS):
                for y0 in range(YS):
                    for c0 in range(CS):
                        source = (((z0 * XS + x0) * HS + h0) * YS + y0) * CS + c0
                        z1, x1, h1 = (z0 + z) % ZS, (x0 + x) % XS, (h0 + h) % HS
                        y1, c1 = (y0 + y) % YS, (c0 + c) % CS
                        pairs.append((source, (((z1 * XS + x1) * HS + h1) * YS + y1) * CS + c1))
    return lax.ppermute(value, AXES, pairs)


def product(left, right):
    return jnp.dot(left, right, preferred_element_type=F32)


def product_right_t(left, right):
    return lax.dot_general(left, right, (((1,), (1,)), ((), ())), preferred_element_type=F32)


def product_left_t(left, right):
    return lax.dot_general(left, right, (((0,), (0,)), ((), ())), preferred_element_type=F32)


def rounded(value):
    return lax.reduce_precision(value, 8, 7)


def parts_of(value, count):
    parts = []
    for _ in range(count):
        top = rounded(value)
        parts.append(top.astype(BF16))
        value = value - top
    return parts


def gather_tokens(own, z, x):
    n = own.shape[1]
    over_y = {0: own}
    for dy in (1, 3, 2):
        over_y[-dy % YS] = send(own, y=dy)
    core = jnp.zeros((256, n), own.dtype)
    for dy in range(YS):
        core = lax.dynamic_update_slice(core, over_y[dy], ((dy - x) % XS * 64, 0))
    other = send(core, c=1)
    both = jnp.zeros((512, n), own.dtype)
    both = lax.dynamic_update_slice(both, core, (z * 256, 0))
    return lax.dynamic_update_slice(both, other, ((1 - z) * 256, 0)), over_y[3]


def sum_over_row(near, arrived):
    m12, a10 = arrived
    a02 = near[2] + m12
    h = a02.shape[0] // 2
    n1 = send(a02[:h].astype(BF16), x=1).astype(F32)
    n2 = send(a02[h:].astype(BF16), x=3).astype(F32)
    q = send(a10.astype(BF16), z=1).astype(F32)
    a01 = jnp.concatenate([near[1][:h] + n1, near[1][h:]], axis=0)
    a03 = jnp.concatenate([near[3][:h], near[3][h:] + n2], axis=0)
    r1 = send(a01.astype(BF16), x=1).astype(F32)
    r2 = send(a03.astype(BF16), x=3).astype(F32)
    return near[0] + q + r1 + r2


def first_step(far, messages):
    m12 = send(messages[2], z=1).astype(F32)
    m11 = send(messages[1], x=1).astype(F32)
    m13 = send(messages[3], x=3).astype(F32)
    return m12, far[0] + m11 + m13


def gather_over_row(own):
    h = own.shape[0] // 2
    a = send(own, x=1)
    b = send(own, x=3)
    p = send(own, z=1)
    a2 = send(a[:h], x=1)
    b2 = send(b[h:], x=3)
    pa = send(p, x=1)
    pb = send(p, x=3)
    across = jnp.concatenate([a2, b2], axis=0)
    p2 = send(across, z=1)
    return (
        jnp.concatenate([own, b, across, a], axis=0),
        jnp.concatenate([p, pb, p2, pa], axis=0),
    )


def sum_over_core_y(partial, gain_partial, z, x):
    give = lax.dynamic_slice(partial, ((1 - z) * 256, 0), (256, 2048))
    give = jnp.concatenate([give, jnp.pad(gain_partial, ((0, 0), (0, 2048 - 128)))], axis=0)
    taken = send(give, c=1)
    keep = lax.dynamic_slice(partial, (z * 256, 0), (256, 2048)) + taken[:256]
    gain = gain_partial + taken[256:, :128]
    gain_parts = jnp.concatenate(parts_of(gain, 2) + [jnp.zeros((48, 128), BF16)], axis=0)

    def gain_of(parts):
        return parts[:8].astype(F32) + parts[8:16].astype(F32)

    def piece(dy):
        return lax.dynamic_slice(keep, ((dy - x) % XS * 64, 0), (64, 2048))

    total = piece(0)
    gains = {0: gain_of(gain_parts)}
    for dy in (1, 3, 2):
        message = jnp.concatenate([piece(dy).astype(BF16), gain_parts], axis=1)
        got = send(message, y=dy)
        total = total + got[:, :2048].astype(F32)
        gains[dy] = gain_of(got[:, 2048:])
    gain = (gains[0] + gains[2]) + (gains[1] + gains[3])
    return total, gain


def per_device(inputs, rms_gain_vector, gate_weight, up_weight, down_weight, out_grad):
    z, x = lax.axis_index("z"), lax.axis_index("x")
    row = z * XS + x
    width = gate_weight.shape[1]

    value_entries = inputs.astype(F32)
    inverse_rms = lax.rsqrt(jnp.mean(value_entries * value_entries, axis=1, keepdims=True) + EPS)
    side = jnp.concatenate(parts_of(inverse_rms, 3) + [jnp.zeros((4, 125), BF16)], axis=1)
    message = jnp.concatenate(
        [
            inputs.reshape(4, 8, 1024),
            jnp.broadcast_to(side[:, None, :], (4, 8, 128)),
            out_grad.reshape(4, 8, 1024),
        ],
        axis=2,
    )
    message = jnp.broadcast_to(jnp.transpose(message, (1, 0, 2))[:, None], (8, HS, 4, 2176))
    block = lax.all_to_all(
        message.reshape(16, 4, 2176), ("z", "x", "h"), split_axis=0, concat_axis=0, tiled=True
    )
    block = block.reshape(64, 2176)
    tokens, first = gather_tokens(block[:, :1152], z, x)
    grad_block, _ = lax.optimization_barrier((block[:, 1152:], first))
    grad_full, _ = gather_tokens(grad_block, z, x)

    inverse_full = (
        tokens[:, 1024:1025].astype(F32)
        + tokens[:, 1025:1026].astype(F32)
        + tokens[:, 1026:1027].astype(F32)
    )
    gain_block = lax.dynamic_slice(rms_gain_vector, (row * 1024,), (1024,))
    estimate = tokens[:, :1024].astype(F32) * inverse_full
    normed = (estimate * gain_block).astype(BF16)

    def gate_up(normed):
        both = [product(normed, gate_weight), product(normed, up_weight)]
        return jnp.concatenate(both, axis=1).reshape(4, 64, 2 * width)

    def for_hidden(grad):
        return product_right_t(grad, down_weight).reshape(4, 64, width)

    far = gate_up(normed[256:])
    messages = [far[i].astype(BF16) for i in range(XS)]
    far_grad = for_hidden(grad_full[256:])
    grad_messages = [far_grad[i].astype(BF16) for i in range(XS)]
    normed_near, grad_near, *messages = lax.optimization_barrier(
        (normed[:256], grad_full[:256], *messages)
    )
    arrived = first_step(far, messages)
    arrived_grad = first_step(far_grad, grad_messages)
    near = jnp.concatenate([gate_up(normed_near), for_hidden(grad_near)], axis=2)
    sums = sum_over_row(
        near, [jnp.concatenate(pair, axis=1) for pair in zip(arrived, arrived_grad, strict=True)]
    )
    gate, up, hidden_grad = sums[:, :width], sums[:, width : 2 * width], sums[:, 2 * width :]
    sigma = jax.nn.sigmoid(gate)
    silu = gate * sigma
    units = jnp.concatenate(
        [
            (silu * up).astype(BF16),
            (hidden_grad * up * sigma * (1.0 + gate * (1.0 - sigma))).astype(BF16),
            (hidden_grad * silu).astype(BF16),
        ],
        axis=1,
    )
    units = gather_over_row(units)

    def backward(units):
        hidden, gate_grad, up_grad = units[:, :width], units[:, width : 2 * width], units[:, 2 * width :]
        grad = product_right_t(gate_grad, gate_weight) + product_right_t(up_grad, up_weight)
        return jnp.concatenate([product(hidden, down_weight), grad], axis=1)

    partial = jnp.concatenate([backward(units[0]), backward(units[1])], axis=0)
    gain_partial = jnp.sum(partial[:, 1024:] * estimate, axis=0).reshape(8, 128)
    total, gain = sum_over_core_y(partial, gain_partial, z, x)
    units = jnp.concatenate(units, axis=0)
    hidden, gate_grad, up_grad = units[:, :width], units[:, width : 2 * width], units[:, 2 * width :]
    down_weight_grad = product_left_t(hidden, grad_full).astype(BF16)
    gate_weight_grad = product_left_t(normed, gate_grad).astype(BF16)
    up_weight_grad = product_left_t(normed, up_grad).astype(BF16)
    total, down_weight_grad, gate_weight_grad = lax.optimization_barrier(
        (total, down_weight_grad, gate_weight_grad)
    )
    gain_parts = [p.reshape(4, 256) for p in parts_of(gain, 2)]
    gain_rows = jnp.broadcast_to(jnp.concatenate(gain_parts, axis=1)[None], (16, 4, 512))
    message = total.astype(BF16).reshape(16, 4, 2048)
    message = jnp.concatenate([message, gain_rows], axis=2)
    back = lax.all_to_all(message, ("z", "x", "h"), split_axis=0, concat_axis=0, tiled=True)
    back = back.reshape(8, HS, 4, 2560).astype(F32)
    gain_grad = back[..., 2048:2304] + back[..., 2304:]
    gain_grad = (gain_grad[:, 0] + gain_grad[:, 1]).reshape(8192)
    back = back[:, 0, :, :2048] + back[:, 1, :, :2048]
    outputs = jnp.transpose(back[..., :1024].astype(BF16), (1, 0, 2)).reshape(4, 8192)
    normed_grad = jnp.transpose(back[..., 1024:], (1, 0, 2)).reshape(4, 8192)

    normalized = value_entries * inverse_rms
    scaled = normed_grad * rms_gain_vector
    input_gradient = inverse_rms * (
        scaled - normalized * jnp.mean(scaled * normalized, axis=1, keepdims=True)
    )
    return (
        outputs,
        input_gradient.astype(BF16),
        gain_grad,
        gate_weight_grad,
        up_weight_grad,
        down_weight_grad,
    )


def solution(mesh):
    fine = Mesh(mesh.devices.reshape(ZS, XS, HS, YS, CS), AXES)
    row, col = AXES[:2], AXES[2:]
    in_specs = (P(AXES, None), P(), P(row, col), P(row, col), P(col, row), P(AXES, None))
    out_specs = (P(AXES, None), P(AXES, None), P(), P(row, col), P(row, col), P(col, row))
    return jax.shard_map(
        per_device, mesh=fine, in_specs=in_specs, out_specs=out_specs, check_vma=False
    )
```

```python
import jax
import jax.numpy as jnp
from jax import lax
from jax.sharding import Mesh, PartitionSpec as P

EPS = 1e-05
F32 = jnp.float32
BF16 = jnp.bfloat16
ZS, XS, HS, YS, CS = 2, 4, 2, 4, 2
AXES = ("z", "x", "h", "y", "core")


def send(value, z=0, x=0, h=0, y=0, c=0):
    pairs = []
    for z0 in range(ZS):
        for x0 in range(XS):
            for h0 in range(HS):
                for y0 in range(YS):
                    for c0 in range(CS):
                        source = (((z0 * XS + x0) * HS + h0) * YS + y0) * CS + c0
                        z1, x1, h1 = (z0 + z) % ZS, (x0 + x) % XS, (h0 + h) % HS
                        y1, c1 = (y0 + y) % YS, (c0 + c) % CS
                        pairs.append((source, (((z1 * XS + x1) * HS + h1) * YS + y1) * CS + c1))
    return lax.ppermute(value, AXES, pairs)


def product(left, right):
    return jnp.dot(left, right, preferred_element_type=F32)


def product_right_t(left, right):
    return lax.dot_general(left, right, (((1,), (1,)), ((), ())), preferred_element_type=F32)


def product_left_t(left, right):
    return lax.dot_general(left, right, (((0,), (0,)), ((), ())), preferred_element_type=F32)


def rounded(value):
    return lax.reduce_precision(value, 8, 7)


def parts_of(value, count):
    parts = []
    for _ in range(count):
        top = rounded(value)
        parts.append(top.astype(BF16))
        value = value - top
    return parts


def gather_half(own, x):
    n = own.shape[1]
    over_y = {0: own}
    for dy in (1, 3, 2):
        over_y[-dy % YS] = send(own, y=dy)
    core = jnp.zeros((128, n), own.dtype)
    for dy in range(YS):
        core = lax.dynamic_update_slice(core, over_y[dy], ((dy - x) % XS * 32, 0))
    return core, over_y[3]


def both_cores(core):
    both = (core, send(core, c=1))
    return jnp.concatenate([v[i * 32 : i * 32 + 32] for i in range(XS) for v in both], axis=0)


def sum_over_core(partial, gain_partial):
    n = partial.shape[1]
    split = [partial[i * 32 : i * 32 + 32] for i in range(2 * XS)]
    give = split[1::2]
    if gain_partial is not None:
        give = give + [jnp.pad(gain_partial, ((0, 0), (0, n - 128)))]
    taken = send(jnp.concatenate(give, axis=0), c=1)
    keep = jnp.concatenate(split[::2], axis=0) + taken[:128]
    if gain_partial is not None:
        gain_partial = gain_partial + taken[128:, :128]
    return keep, gain_partial


def sum_over_y(keep, gain, x):
    n = keep.shape[1]

    def piece(dy):
        return lax.dynamic_slice(keep, ((dy - x) % XS * 32, 0), (32, n))

    def gain_of(parts):
        return parts[:8].astype(F32) + parts[8:16].astype(F32)

    if gain is not None:
        parts = jnp.concatenate(parts_of(gain, 2) + [jnp.zeros((16, 128), BF16)], axis=0)
        gains = {0: gain_of(parts)}
    total = piece(0)
    for dy in (1, 3, 2):
        message = piece(dy).astype(BF16)
        if gain is not None:
            message = jnp.concatenate([message, parts], axis=1)
        got = send(message, y=dy)
        total = total + got[:, :n].astype(F32)
        if gain is not None:
            gains[dy] = gain_of(got[:, n:])
    if gain is not None:
        gain = (gains[0] + gains[2]) + (gains[1] + gains[3])
    return total, gain


def sum_over_row(near, far):
    m12 = send(far[2].astype(BF16), z=1).astype(F32)
    m11 = send(far[1].astype(BF16), x=1).astype(F32)
    m13 = send(far[3].astype(BF16), x=3).astype(F32)
    a02 = near[2] + m12
    h = a02.shape[0] // 2
    n1 = send(a02[:h].astype(BF16), x=1).astype(F32)
    n2 = send(a02[h:].astype(BF16), x=3).astype(F32)
    q = send((far[0] + m11 + m13).astype(BF16), z=1).astype(F32)
    a01 = jnp.concatenate([near[1][:h] + n1, near[1][h:]], axis=0)
    a03 = jnp.concatenate([near[3][:h], near[3][h:] + n2], axis=0)
    r1 = send(a01.astype(BF16), x=1).astype(F32)
    r2 = send(a03.astype(BF16), x=3).astype(F32)
    return near[0] + q + r1 + r2


def gather_over_row(own):
    h = own.shape[0] // 2
    a = send(own, x=1)
    b = send(own, x=3)
    p = send(own, z=1)
    a2 = send(a[:h], x=1)
    b2 = send(b[h:], x=3)
    pa = send(p, x=1)
    pb = send(p, x=3)
    across = jnp.concatenate([a2, b2], axis=0)
    p2 = send(across, z=1)
    return (
        jnp.concatenate([own, b, across, a], axis=0),
        jnp.concatenate([p, pb, p2, pa], axis=0),
    )


def per_device(inputs, rms_gain_vector, gate_weight, up_weight, down_weight, out_grad):
    z, x = lax.axis_index("z"), lax.axis_index("x")
    row = z * XS + x
    width = gate_weight.shape[1]

    value_entries = inputs.astype(F32)
    inverse_rms = lax.rsqrt(jnp.mean(value_entries * value_entries, axis=1, keepdims=True) + EPS)
    side = jnp.concatenate(parts_of(inverse_rms, 3) + [jnp.zeros((4, 125), BF16)], axis=1)
    message = jnp.concatenate(
        [
            inputs.reshape(4, 8, 1024),
            out_grad.reshape(4, 8, 1024),
            jnp.broadcast_to(side[:, None, :], (4, 8, 128)),
        ],
        axis=2,
    )
    message = jnp.broadcast_to(jnp.transpose(message, (1, 0, 2))[None], (HS, 8, 4, 2176))
    block = lax.all_to_all(
        message.reshape(16, 4, 2176), ("h", "z", "x"), split_axis=0, concat_axis=0, tiled=True
    )
    block = block.reshape(64, 2176)
    gain_block = lax.dynamic_slice(rms_gain_vector, (row * 1024,), (1024,))

    def normed_of(tokens):
        inverse = (
            tokens[:, 2048:2049].astype(F32)
            + tokens[:, 2049:2050].astype(F32)
            + tokens[:, 2050:2051].astype(F32)
        )
        estimate = tokens[:, :1024].astype(F32) * inverse
        return estimate, (estimate * gain_block).astype(BF16), tokens[:, 1024:2048]

    def partials(normed, grad):
        return jnp.concatenate(
            [
                product(normed, gate_weight),
                product(normed, up_weight),
                product_right_t(grad, down_weight),
            ],
            axis=1,
        ).reshape(4, 64, 3 * width)

    far_core, first = gather_half(lax.dynamic_slice(block, ((1 - z) * 32, 0), (32, 2176)), x)
    near_block, _ = lax.optimization_barrier(
        (lax.dynamic_slice(block, (z * 32, 0), (32, 2176)), first)
    )
    near_core, _ = gather_half(near_block, x)
    far_estimate, far_normed, far_grad = normed_of(both_cores(far_core))
    far = partials(far_normed, far_grad)
    near_core, far = lax.optimization_barrier((near_core, far))
    near_estimate, near_normed, near_grad = normed_of(both_cores(near_core))
    near = partials(near_normed, near_grad)
    sums = sum_over_row(near, far)
    gate, up, hidden_grad = sums[:, :width], sums[:, width : 2 * width], sums[:, 2 * width :]
    sigma = jax.nn.sigmoid(gate)
    silu = gate * sigma
    units = jnp.concatenate(
        [
            (silu * up).astype(BF16),
            (hidden_grad * up * sigma * (1.0 + gate * (1.0 - sigma))).astype(BF16),
            (hidden_grad * silu).astype(BF16),
        ],
        axis=1,
    )
    units = gather_over_row(units)

    def backward(units):
        hidden, gate_grad, up_grad = units[:, :width], units[:, width : 2 * width], units[:, 2 * width :]
        grad = product_right_t(gate_grad, gate_weight) + product_right_t(up_grad, up_weight)
        return jnp.concatenate([product(hidden, down_weight), grad], axis=1)

    near_partial = backward(units[0])
    near_total, _ = sum_over_y(sum_over_core(near_partial, None)[0], None, x)
    far_partial = backward(units[1])
    gain_partial = jnp.sum(near_partial[:, 1024:] * near_estimate, axis=0) + jnp.sum(
        far_partial[:, 1024:] * far_estimate, axis=0
    )
    far_total, gain = sum_over_y(*sum_over_core(far_partial, gain_partial.reshape(8, 128)), x)

    units = jnp.concatenate(units, axis=0)
    hidden, gate_grad, up_grad = units[:, :width], units[:, width : 2 * width], units[:, 2 * width :]
    normed = jnp.concatenate([near_normed, far_normed], axis=0)
    grad_full = jnp.concatenate([near_grad, far_grad], axis=0)
    down_weight_grad = product_left_t(hidden, grad_full).astype(BF16)
    gate_weight_grad = product_left_t(normed, gate_grad).astype(BF16)
    up_weight_grad = product_left_t(normed, up_grad).astype(BF16)
    far_total, down_weight_grad, gate_weight_grad = lax.optimization_barrier(
        (far_total, down_weight_grad, gate_weight_grad)
    )

    gain_parts = [p.reshape(4, 256) for p in parts_of(gain, 2)]
    gain_rows = jnp.broadcast_to(jnp.concatenate(gain_parts, axis=1)[None], (16, 4, 512))
    total = jnp.zeros((64, 2048), BF16)
    total = lax.dynamic_update_slice(total, near_total.astype(BF16), (z * 32, 0))
    total = lax.dynamic_update_slice(total, far_total.astype(BF16), ((1 - z) * 32, 0))
    message = jnp.concatenate([total.reshape(16, 4, 2048), gain_rows], axis=2)
    back = lax.all_to_all(message, ("h", "z", "x"), split_axis=0, concat_axis=0, tiled=True)
    back = back.reshape(HS, 8, 4, 2560).astype(F32)
    gain_grad = back[..., 2048:2304] + back[..., 2304:]
    gain_grad = (gain_grad[0] + gain_grad[1]).reshape(8192)
    back = back[0, :, :, :2048] + back[1, :, :, :2048]
    outputs = jnp.transpose(back[..., :1024].astype(BF16), (1, 0, 2)).reshape(4, 8192)
    normed_grad = jnp.transpose(back[..., 1024:], (1, 0, 2)).reshape(4, 8192)

    normalized = value_entries * inverse_rms
    scaled = normed_grad * rms_gain_vector
    input_gradient = inverse_rms * (
        scaled - normalized * jnp.mean(scaled * normalized, axis=1, keepdims=True)
    )
    return (
        outputs,
        input_gradient.astype(BF16),
        gain_grad,
        gate_weight_grad,
        up_weight_grad,
        down_weight_grad,
    )


def solution(mesh):
    fine = Mesh(mesh.devices.reshape(ZS, XS, HS, YS, CS), AXES)
    row, col = AXES[:2], AXES[2:]
    in_specs = (P(AXES, None), P(), P(row, col), P(row, col), P(col, row), P(AXES, None))
    out_specs = (P(AXES, None), P(AXES, None), P(), P(row, col), P(row, col), P(col, row))
    return jax.shard_map(
        per_device, mesh=fine, in_specs=in_specs, out_specs=out_specs, check_vma=False
    )
```

```python
import jax
import jax.numpy as jnp
from jax import lax
from jax.sharding import Mesh, PartitionSpec as P

EPS = 1e-05
F32 = jnp.float32
BF16 = jnp.bfloat16
ZS, XS, HS, YS, CS = 2, 4, 2, 4, 2
AXES = ("z", "x", "h", "y", "core")


def send(value, z=0, x=0, h=0, y=0, c=0):
    pairs = []
    for z0 in range(ZS):
        for x0 in range(XS):
            for h0 in range(HS):
                for y0 in range(YS):
                    for c0 in range(CS):
                        source = (((z0 * XS + x0) * HS + h0) * YS + y0) * CS + c0
                        z1, x1, h1 = (z0 + z) % ZS, (x0 + x) % XS, (h0 + h) % HS
                        y1, c1 = (y0 + y) % YS, (c0 + c) % CS
                        pairs.append((source, (((z1 * XS + x1) * HS + h1) * YS + y1) * CS + c1))
    return lax.ppermute(value, AXES, pairs)


def product(left, right):
    return jnp.dot(left, right, preferred_element_type=F32)


def product_right_t(left, right):
    return lax.dot_general(left, right, (((1,), (1,)), ((), ())), preferred_element_type=F32)


def product_left_t(left, right):
    return lax.dot_general(left, right, (((0,), (0,)), ((), ())), preferred_element_type=F32)


def rounded(value):
    return lax.reduce_precision(value, 8, 7)


def parts_of(value, count):
    parts = []
    for _ in range(count):
        top = rounded(value)
        parts.append(top.astype(BF16))
        value = value - top
    return parts


def gather_half(own, x):
    n = own.shape[1]
    over_y = {0: own}
    for dy in (1, 3, 2):
        over_y[-dy % YS] = send(own, y=dy)
    core = jnp.zeros((128, n), own.dtype)
    for dy in range(YS):
        core = lax.dynamic_update_slice(core, over_y[dy], ((dy - x) % XS * 32, 0))
    return core, over_y[3]


def both_cores(core):
    both = (core, send(core, c=1))
    return jnp.concatenate([v[i * 32 : i * 32 + 32] for i in range(XS) for v in both], axis=0)


def sum_over_core(partial, gain_partial):
    n = partial.shape[1]
    split = [partial[i * 32 : i * 32 + 32] for i in range(2 * XS)]
    give = split[1::2]
    if gain_partial is not None:
        give = give + [jnp.pad(gain_partial, ((0, 0), (0, n - 128)))]
    taken = send(jnp.concatenate(give, axis=0), c=1)
    keep = jnp.concatenate(split[::2], axis=0) + taken[:128]
    if gain_partial is not None:
        gain_partial = gain_partial + taken[128:, :128]
    return keep, gain_partial


def sum_over_y(keep, gain, x):
    n = keep.shape[1]

    def piece(dy):
        return lax.dynamic_slice(keep, ((dy - x) % XS * 32, 0), (32, n))

    def gain_of(parts):
        return parts[:8].astype(F32) + parts[8:16].astype(F32)

    if gain is not None:
        parts = jnp.concatenate(parts_of(gain, 2) + [jnp.zeros((16, 128), BF16)], axis=0)
        gains = {0: gain_of(parts)}
    total = piece(0)
    for dy in (1, 3, 2):
        message = piece(dy).astype(BF16)
        if gain is not None:
            message = jnp.concatenate([message, parts], axis=1)
        got = send(message, y=dy)
        total = total + got[:, :n].astype(F32)
        if gain is not None:
            gains[dy] = gain_of(got[:, n:])
    if gain is not None:
        gain = (gains[0] + gains[2]) + (gains[1] + gains[3])
    return total, gain


def sum_over_row(near, far):
    m12 = send(far[2].astype(BF16), z=1).astype(F32)
    m11 = send(far[1].astype(BF16), x=1).astype(F32)
    m13 = send(far[3].astype(BF16), x=3).astype(F32)
    h = near[0].shape[0] // 2
    first1 = send(near[1][h:].astype(BF16), x=1)
    first2 = send(near[3][:h].astype(BF16), x=3)
    a02 = near[2] + m12
    n1 = send(a02[:h].astype(BF16), x=1).astype(F32)
    n2 = send(a02[h:].astype(BF16), x=3).astype(F32)
    q = send((far[0] + m11 + m13).astype(BF16), z=1).astype(F32)
    last1 = (near[1][:h] + n1).astype(BF16)
    last2 = (near[3][h:] + n2).astype(BF16)
    last1, last2, first1, first2 = lax.optimization_barrier((last1, last2, first1, first2))
    r1 = jnp.concatenate([send(last1, x=1), first1], axis=0).astype(F32)
    r2 = jnp.concatenate([first2, send(last2, x=3)], axis=0).astype(F32)
    return near[0] + q + r1 + r2


def gather_over_row(own):
    h = own.shape[0] // 2
    a = send(own, x=1)
    b = send(own, x=3)
    p = send(own, z=1)
    a2 = send(a[:h], x=1)
    b2 = send(b[h:], x=3)
    pa = send(p, x=1)
    pb = send(p, x=3)
    across = jnp.concatenate([a2, b2], axis=0)
    p2 = send(across, z=1)
    return (
        jnp.concatenate([own, b, across, a], axis=0),
        jnp.concatenate([p, pb, p2, pa], axis=0),
    )


def per_device(inputs, rms_gain_vector, gate_weight, up_weight, down_weight, out_grad):
    z, x = lax.axis_index("z"), lax.axis_index("x")
    row = z * XS + x
    width = gate_weight.shape[1]

    value_entries = inputs.astype(F32)
    inverse_rms = lax.rsqrt(jnp.mean(value_entries * value_entries, axis=1, keepdims=True) + EPS)
    side = jnp.concatenate(parts_of(inverse_rms, 3) + [jnp.zeros((4, 125), BF16)], axis=1)
    message = jnp.concatenate(
        [
            inputs.reshape(4, 8, 1024),
            out_grad.reshape(4, 8, 1024),
            jnp.broadcast_to(side[:, None, :], (4, 8, 128)),
        ],
        axis=2,
    )
    message = jnp.broadcast_to(jnp.transpose(message, (1, 0, 2))[None], (HS, 8, 4, 2176))
    block = lax.all_to_all(
        message.reshape(16, 4, 2176), ("h", "z", "x"), split_axis=0, concat_axis=0, tiled=True
    )
    block = block.reshape(64, 2176)
    gain_block = lax.dynamic_slice(rms_gain_vector, (row * 1024,), (1024,))

    def normed_of(tokens):
        inverse = (
            tokens[:, 2048:2049].astype(F32)
            + tokens[:, 2049:2050].astype(F32)
            + tokens[:, 2050:2051].astype(F32)
        )
        estimate = tokens[:, :1024].astype(F32) * inverse
        return estimate, (estimate * gain_block).astype(BF16), tokens[:, 1024:2048]

    def partials(normed, grad):
        return jnp.concatenate(
            [
                product(normed, gate_weight),
                product(normed, up_weight),
                product_right_t(grad, down_weight),
            ],
            axis=1,
        ).reshape(4, 64, 3 * width)

    far_core, first = gather_half(lax.dynamic_slice(block, ((1 - z) * 32, 0), (32, 2176)), x)
    near_block, _ = lax.optimization_barrier(
        (lax.dynamic_slice(block, (z * 32, 0), (32, 2176)), first)
    )
    near_core, _ = gather_half(near_block, x)
    far_estimate, far_normed, far_grad = normed_of(both_cores(far_core))
    far = partials(far_normed, far_grad)
    near_core, far = lax.optimization_barrier((near_core, far))
    near_estimate, near_normed, near_grad = normed_of(both_cores(near_core))
    near = partials(near_normed, near_grad)
    sums = sum_over_row(near, far)
    gate, up, hidden_grad = sums[:, :width], sums[:, width : 2 * width], sums[:, 2 * width :]
    sigma = jax.nn.sigmoid(gate)
    silu = gate * sigma
    units = jnp.concatenate(
        [
            (silu * up).astype(BF16),
            (hidden_grad * up * sigma * (1.0 + gate * (1.0 - sigma))).astype(BF16),
            (hidden_grad * silu).astype(BF16),
        ],
        axis=1,
    )
    units = gather_over_row(units)

    def backward(units):
        hidden, gate_grad, up_grad = units[:, :width], units[:, width : 2 * width], units[:, 2 * width :]
        grad = product_right_t(gate_grad, gate_weight) + product_right_t(up_grad, up_weight)
        return jnp.concatenate([product(hidden, down_weight), grad], axis=1)

    near_partial = backward(units[0])
    near_keep, _ = sum_over_core(near_partial, None)
    near_total, _ = sum_over_y(near_keep, None, x)
    far_units, near_total = lax.optimization_barrier((units[1], near_total))
    far_partial = backward(far_units)
    gain_partial = jnp.sum(near_partial[:, 1024:] * near_estimate, axis=0) + jnp.sum(
        far_partial[:, 1024:] * far_estimate, axis=0
    )
    far_keep, gain = sum_over_core(far_partial, gain_partial.reshape(8, 128))

    units = jnp.concatenate([units[0], far_units], axis=0)
    hidden, gate_grad, up_grad = units[:, :width], units[:, width : 2 * width], units[:, 2 * width :]
    normed = jnp.concatenate([near_normed, far_normed], axis=0)
    grad_full = jnp.concatenate([near_grad, far_grad], axis=0)
    down_weight_grad = product_left_t(hidden, grad_full).astype(BF16)
    far_keep, down_weight_grad = lax.optimization_barrier((far_keep, down_weight_grad))
    far_total, gain = sum_over_y(far_keep, gain, x)
    normed, far_total = lax.optimization_barrier((normed, far_total))
    gate_weight_grad = product_left_t(normed, gate_grad).astype(BF16)
    up_weight_grad = product_left_t(normed, up_grad).astype(BF16)

    gain_parts = [p.reshape(4, 256) for p in parts_of(gain, 2)]
    gain_rows = jnp.broadcast_to(jnp.concatenate(gain_parts, axis=1)[None], (16, 4, 512))
    total = jnp.zeros((64, 2048), BF16)
    total = lax.dynamic_update_slice(total, near_total.astype(BF16), (z * 32, 0))
    total = lax.dynamic_update_slice(total, far_total.astype(BF16), ((1 - z) * 32, 0))
    message = jnp.concatenate([total.reshape(16, 4, 2048), gain_rows], axis=2)
    back = lax.all_to_all(message, ("h", "z", "x"), split_axis=0, concat_axis=0, tiled=True)
    back = back.reshape(HS, 8, 4, 2560).astype(F32)
    gain_grad = back[..., 2048:2304] + back[..., 2304:]
    gain_grad = (gain_grad[0] + gain_grad[1]).reshape(8192)
    back = back[0, :, :, :2048] + back[1, :, :, :2048]
    outputs = jnp.transpose(back[..., :1024].astype(BF16), (1, 0, 2)).reshape(4, 8192)
    normed_grad = jnp.transpose(back[..., 1024:], (1, 0, 2)).reshape(4, 8192)

    normalized = value_entries * inverse_rms
    scaled = normed_grad * rms_gain_vector
    input_gradient = inverse_rms * (
        scaled - normalized * jnp.mean(scaled * normalized, axis=1, keepdims=True)
    )
    return (
        outputs,
        input_gradient.astype(BF16),
        gain_grad,
        gate_weight_grad,
        up_weight_grad,
        down_weight_grad,
    )


def solution(mesh):
    fine = Mesh(mesh.devices.reshape(ZS, XS, HS, YS, CS), AXES)
    row, col = AXES[:2], AXES[2:]
    in_specs = (P(AXES, None), P(), P(row, col), P(row, col), P(col, row), P(AXES, None))
    out_specs = (P(AXES, None), P(AXES, None), P(), P(row, col), P(row, col), P(col, row))
    return jax.shard_map(
        per_device, mesh=fine, in_specs=in_specs, out_specs=out_specs, check_vma=False
    )
```

```python
import jax
import jax.numpy as jnp
from jax import lax
from jax.sharding import Mesh, PartitionSpec as P

EPS = 1e-05
F32 = jnp.float32
BF16 = jnp.bfloat16
ZS, XS, HS, YS, CS = 2, 4, 2, 4, 2
AXES = ("z", "x", "h", "y", "core")


def send(value, z=0, x=0, h=0, y=0, c=0):
    pairs = []
    for z0 in range(ZS):
        for x0 in range(XS):
            for h0 in range(HS):
                for y0 in range(YS):
                    for c0 in range(CS):
                        source = (((z0 * XS + x0) * HS + h0) * YS + y0) * CS + c0
                        z1, x1, h1 = (z0 + z) % ZS, (x0 + x) % XS, (h0 + h) % HS
                        y1, c1 = (y0 + y) % YS, (c0 + c) % CS
                        pairs.append((source, (((z1 * XS + x1) * HS + h1) * YS + y1) * CS + c1))
    return lax.ppermute(value, AXES, pairs)


def product(left, right):
    return jnp.dot(left, right, preferred_element_type=F32)


def product_right_t(left, right):
    return lax.dot_general(left, right, (((1,), (1,)), ((), ())), preferred_element_type=F32)


def product_left_t(left, right):
    return lax.dot_general(left, right, (((0,), (0,)), ((), ())), preferred_element_type=F32)


def rounded(value):
    return lax.reduce_precision(value, 8, 7)


def parts_of(value, count):
    parts = []
    for _ in range(count):
        top = rounded(value)
        parts.append(top.astype(BF16))
        value = value - top
    return parts


def gather_half(own, x):
    n = own.shape[1]
    over_y = {0: own}
    for dy in (1, 3, 2):
        over_y[-dy % YS] = send(own, y=dy)
    core = jnp.zeros((128, n), own.dtype)
    for dy in range(YS):
        core = lax.dynamic_update_slice(core, over_y[dy], ((dy - x) % XS * 32, 0))
    return core


def both_cores(core):
    both = (core, send(core, c=1))
    return jnp.concatenate([v[i * 32 : i * 32 + 32] for i in range(XS) for v in both], axis=0)


def sum_over_core(near, far, gain):
    n = near.shape[1]

    def rows_of(core):
        return [
            half[i * 64 + core * 32 : i * 64 + core * 32 + 32]
            for i in range(XS)
            for half in (near, far)
        ]

    gain_rows = jnp.pad(gain, ((0, 0), (0, n - 128)))
    taken = send(jnp.concatenate(rows_of(1) + [gain_rows], axis=0), c=1)
    return jnp.concatenate(rows_of(0), axis=0) + taken[:256], gain + taken[256:, :128]


def sum_over_y(keep, gain, x):
    n = keep.shape[1]

    def piece(dy):
        return lax.dynamic_slice(keep, ((dy - x) % XS * 64, 0), (64, n))

    def gain_of(parts):
        return parts[:8].astype(F32) + parts[8:16].astype(F32)

    parts = jnp.concatenate(parts_of(gain, 2) + [jnp.zeros((48, 128), BF16)], axis=0)
    gains = {0: gain_of(parts)}
    total = piece(0)
    for dy in (1, 3, 2):
        got = send(jnp.concatenate([piece(dy).astype(BF16), parts], axis=1), y=dy)
        total = total + got[:, :n].astype(F32)
        gains[dy] = gain_of(got[:, n:])
    return total, (gains[0] + gains[2]) + (gains[1] + gains[3])


def sum_over_row(near, far):
    m12 = send(far[2].astype(BF16), z=1).astype(F32)
    m11 = send(far[1].astype(BF16), x=1).astype(F32)
    m13 = send(far[3].astype(BF16), x=3).astype(F32)
    h = near[0].shape[0] // 2
    first1 = send(near[1][h:].astype(BF16), x=1)
    first2 = send(near[3][:h].astype(BF16), x=3)
    a02 = near[2] + m12
    n1 = send(a02[:h].astype(BF16), x=1).astype(F32)
    n2 = send(a02[h:].astype(BF16), x=3).astype(F32)
    q = send((far[0] + m11 + m13).astype(BF16), z=1).astype(F32)
    last1 = (near[1][:h] + n1).astype(BF16)
    last2 = (near[3][h:] + n2).astype(BF16)
    last1, last2, first1, first2 = lax.optimization_barrier((last1, last2, first1, first2))
    r1 = jnp.concatenate([send(last1, x=1), first1], axis=0).astype(F32)
    r2 = jnp.concatenate([first2, send(last2, x=3)], axis=0).astype(F32)
    return near[0] + q + r1 + r2


def gather_over_row(own):
    h = own.shape[0] // 2
    a = send(own, x=1)
    b = send(own, x=3)
    p = send(own, z=1)
    a2 = send(a[:h], x=1)
    b2 = send(b[h:], x=3)
    pa = send(p, x=1)
    pb = send(p, x=3)
    across = jnp.concatenate([a2, b2], axis=0)
    p2 = send(across, z=1)
    near = jnp.concatenate([own, b, across, a], axis=0)
    near, pb = lax.optimization_barrier((near, pb))
    return near, jnp.concatenate([p, pb, p2, pa], axis=0)


def per_device(inputs, rms_gain_vector, gate_weight, up_weight, down_weight, out_grad):
    z, x = lax.axis_index("z"), lax.axis_index("x")
    row = z * XS + x
    width = gate_weight.shape[1]

    value_entries = inputs.astype(F32)
    inverse_rms = lax.rsqrt(jnp.mean(value_entries * value_entries, axis=1, keepdims=True) + EPS)
    side = jnp.concatenate(parts_of(inverse_rms, 3) + [jnp.zeros((4, 125), BF16)], axis=1)
    message = jnp.concatenate(
        [
            inputs.reshape(4, 8, 1024),
            out_grad.reshape(4, 8, 1024),
            jnp.broadcast_to(side[:, None, :], (4, 8, 128)),
        ],
        axis=2,
    )
    message = jnp.broadcast_to(jnp.transpose(message, (1, 0, 2))[None], (HS, 8, 4, 2176))
    block = lax.all_to_all(
        message.reshape(16, 4, 2176), ("h", "z", "x"), split_axis=0, concat_axis=0, tiled=True
    )
    block = block.reshape(64, 2176)
    gain_block = lax.dynamic_slice(rms_gain_vector, (row * 1024,), (1024,))

    def normed_of(tokens):
        inverse = (
            tokens[:, 2048:2049].astype(F32)
            + tokens[:, 2049:2050].astype(F32)
            + tokens[:, 2050:2051].astype(F32)
        )
        estimate = tokens[:, :1024].astype(F32) * inverse
        return estimate, (estimate * gain_block).astype(BF16), tokens[:, 1024:2048]

    def partials(normed, grad):
        return jnp.concatenate(
            [
                product(normed, gate_weight),
                product(normed, up_weight),
                product_right_t(grad, down_weight),
            ],
            axis=1,
        ).reshape(4, 64, 3 * width)

    far_core = gather_half(lax.dynamic_slice(block, ((1 - z) * 32, 0), (32, 2176)), x)
    near_block, far_core = lax.optimization_barrier(
        (lax.dynamic_slice(block, (z * 32, 0), (32, 2176)), far_core)
    )
    near_core = gather_half(near_block, x)
    far_estimate, far_normed, far_grad = normed_of(both_cores(far_core))
    far = partials(far_normed, far_grad)
    near_core, far_own = lax.optimization_barrier((near_core, far[0]))
    near_estimate, near_normed, near_grad = normed_of(both_cores(near_core))
    near = partials(near_normed, near_grad)
    sums = sum_over_row(near, [far_own, far[1], far[2], far[3]])
    gate, up, hidden_grad = sums[:, :width], sums[:, width : 2 * width], sums[:, 2 * width :]
    sigma = jax.nn.sigmoid(gate)
    silu = gate * sigma
    units = jnp.concatenate(
        [
            (silu * up).astype(BF16),
            (hidden_grad * up * sigma * (1.0 + gate * (1.0 - sigma))).astype(BF16),
            (hidden_grad * silu).astype(BF16),
        ],
        axis=1,
    )
    units = gather_over_row(units)

    def backward(units):
        hidden, gate_grad, up_grad = units[:, :width], units[:, width : 2 * width], units[:, 2 * width :]
        grad = product_right_t(gate_grad, gate_weight) + product_right_t(up_grad, up_weight)
        return jnp.concatenate([product(hidden, down_weight), grad], axis=1)

    near_partial = backward(units[0])
    far_partial = backward(units[1])
    gain_partial = jnp.sum(near_partial[:, 1024:] * near_estimate, axis=0) + jnp.sum(
        far_partial[:, 1024:] * far_estimate, axis=0
    )
    keep, gain = sum_over_core(near_partial, far_partial, gain_partial.reshape(8, 128))

    units = jnp.concatenate(units, axis=0)
    hidden, gate_grad, up_grad = units[:, :width], units[:, width : 2 * width], units[:, 2 * width :]
    normed = jnp.concatenate([near_normed, far_normed], axis=0)
    grad_full = jnp.concatenate([near_grad, far_grad], axis=0)
    down_weight_grad = product_left_t(hidden, grad_full).astype(BF16)
    keep, down_weight_grad = lax.optimization_barrier((keep, down_weight_grad))
    total, gain = sum_over_y(keep, gain, x)
    normed, total = lax.optimization_barrier((normed, total))
    gate_weight_grad = product_left_t(normed, gate_grad).astype(BF16)
    up_weight_grad = product_left_t(normed, up_grad).astype(BF16)

    gain_parts = [p.reshape(4, 256) for p in parts_of(gain, 2)]
    gain_rows = jnp.broadcast_to(jnp.concatenate(gain_parts, axis=1)[None], (16, 4, 512))
    total = total.astype(BF16)
    total = jnp.where(z == 0, total, jnp.concatenate([total[32:], total[:32]], axis=0))
    message = jnp.concatenate([total.reshape(16, 4, 2048), gain_rows], axis=2)
    back = lax.all_to_all(message, ("h", "z", "x"), split_axis=0, concat_axis=0, tiled=True)
    back = back.reshape(HS, 8, 4, 2560).astype(F32)
    gain_grad = back[..., 2048:2304] + back[..., 2304:]
    gain_grad = (gain_grad[0] + gain_grad[1]).reshape(8192)
    back = back[0, :, :, :2048] + back[1, :, :, :2048]
    outputs = jnp.transpose(back[..., :1024].astype(BF16), (1, 0, 2)).reshape(4, 8192)
    normed_grad = jnp.transpose(back[..., 1024:], (1, 0, 2)).reshape(4, 8192)

    normalized = value_entries * inverse_rms
    scaled = normed_grad * rms_gain_vector
    input_gradient = inverse_rms * (
        scaled - normalized * jnp.mean(scaled * normalized, axis=1, keepdims=True)
    )
    return (
        outputs,
        input_gradient.astype(BF16),
        gain_grad,
        gate_weight_grad,
        up_weight_grad,
        down_weight_grad,
    )


def solution(mesh):
    fine = Mesh(mesh.devices.reshape(ZS, XS, HS, YS, CS), AXES)
    row, col = AXES[:2], AXES[2:]
    in_specs = (P(AXES, None), P(), P(row, col), P(row, col), P(col, row), P(AXES, None))
    out_specs = (P(AXES, None), P(AXES, None), P(), P(row, col), P(row, col), P(col, row))
    return jax.shard_map(
        per_device, mesh=fine, in_specs=in_specs, out_specs=out_specs, check_vma=False
    )
```

```python
import jax
import jax.numpy as jnp
from jax import lax
from jax.sharding import Mesh, PartitionSpec as P

EPS = 1e-05
F32 = jnp.float32
BF16 = jnp.bfloat16
ZS, XS, HS, YS, CS = 2, 4, 2, 4, 2
AXES = ("z", "x", "h", "y", "core")


def send(value, z=0, x=0, h=0, y=0, c=0):
    pairs = []
    for z0 in range(ZS):
        for x0 in range(XS):
            for h0 in range(HS):
                for y0 in range(YS):
                    for c0 in range(CS):
                        source = (((z0 * XS + x0) * HS + h0) * YS + y0) * CS + c0
                        z1, x1, h1 = (z0 + z) % ZS, (x0 + x) % XS, (h0 + h) % HS
                        y1, c1 = (y0 + y) % YS, (c0 + c) % CS
                        pairs.append((source, (((z1 * XS + x1) * HS + h1) * YS + y1) * CS + c1))
    return lax.ppermute(value, AXES, pairs)


def product(left, right):
    return jnp.dot(left, right, preferred_element_type=F32)


def product_right_t(left, right):
    return lax.dot_general(left, right, (((1,), (1,)), ((), ())), preferred_element_type=F32)


def product_left_t(left, right):
    return lax.dot_general(left, right, (((0,), (0,)), ((), ())), preferred_element_type=F32)


def rounded(value):
    return lax.reduce_precision(value, 8, 7)


def parts_of(value, count):
    parts = []
    for _ in range(count):
        top = rounded(value)
        parts.append(top.astype(BF16))
        value = value - top
    return parts


def gather_half(own, x):
    n = own.shape[1]
    over_y = {0: own}
    for dy in (1, 3, 2):
        over_y[-dy % YS] = send(own, y=dy)
    core = jnp.zeros((128, n), own.dtype)
    for dy in range(YS):
        core = lax.dynamic_update_slice(core, over_y[dy], ((dy - x) % XS * 32, 0))
    return core, over_y[3]


def both_cores(core):
    both = (core, send(core, c=1))
    return jnp.concatenate([v[i * 32 : i * 32 + 32] for i in range(XS) for v in both], axis=0)


def sum_over_core(partial, gain_partial):
    n = partial.shape[1]
    split = [partial[i * 32 : i * 32 + 32] for i in range(2 * XS)]
    give = split[1::2]
    if gain_partial is not None:
        give = give + [jnp.pad(gain_partial, ((0, 0), (0, n - 128)))]
    taken = send(jnp.concatenate(give, axis=0), c=1)
    keep = jnp.concatenate(split[::2], axis=0) + taken[:128]
    if gain_partial is not None:
        gain_partial = gain_partial + taken[128:, :128]
    return keep, gain_partial


def sum_over_y(near, far, gain, x):
    n = near.shape[1]

    def piece(dy):
        start = (dy - x) % XS * 32
        halves = [lax.dynamic_slice(half, (start, 0), (32, n)) for half in (near, far)]
        return jnp.concatenate(halves, axis=0)

    def gain_of(parts):
        return parts[:8].astype(F32) + parts[8:16].astype(F32)

    parts = jnp.concatenate(parts_of(gain, 2) + [jnp.zeros((48, 128), BF16)], axis=0)
    gains = {0: gain_of(parts)}
    total = piece(0)
    for dy in (1, 3, 2):
        got = send(jnp.concatenate([piece(dy).astype(BF16), parts], axis=1), y=dy)
        total = total + got[:, :n].astype(F32)
        gains[dy] = gain_of(got[:, n:])
    return total, (gains[0] + gains[2]) + (gains[1] + gains[3])


def sum_over_row(near, far):
    m12 = send(far[2].astype(BF16), z=1).astype(F32)
    m11 = send(far[1].astype(BF16), x=1).astype(F32)
    m13 = send(far[3].astype(BF16), x=3).astype(F32)
    h = near[0].shape[0] // 2
    first1 = send(near[1][h:].astype(BF16), x=1)
    first2 = send(near[3][:h].astype(BF16), x=3)
    a02 = near[2] + m12
    n1 = send(a02[:h].astype(BF16), x=1).astype(F32)
    n2 = send(a02[h:].astype(BF16), x=3).astype(F32)
    q = send((far[0] + m11 + m13).astype(BF16), z=1).astype(F32)
    last1 = (near[1][:h] + n1).astype(BF16)
    last2 = (near[3][h:] + n2).astype(BF16)
    last1, last2, first1, first2 = lax.optimization_barrier((last1, last2, first1, first2))
    r1 = jnp.concatenate([send(last1, x=1), first1], axis=0).astype(F32)
    r2 = jnp.concatenate([first2, send(last2, x=3)], axis=0).astype(F32)
    return near[0] + q + r1 + r2


def gather_over_row(own):
    h = own.shape[0] // 2
    a = send(own, x=1)
    b = send(own, x=3)
    p = send(own, z=1)
    a2 = send(a[:h], x=1)
    b2 = send(b[h:], x=3)
    pa = send(p, x=1)
    pb = send(p, x=3)
    across = jnp.concatenate([a2, b2], axis=0)
    p2 = send(across, z=1)
    return (
        jnp.concatenate([own, b, across, a], axis=0),
        jnp.concatenate([p, pb, p2, pa], axis=0),
    )


def per_device(inputs, rms_gain_vector, gate_weight, up_weight, down_weight, out_grad):
    z, x = lax.axis_index("z"), lax.axis_index("x")
    row = z * XS + x
    width = gate_weight.shape[1]

    value_entries = inputs.astype(F32)
    inverse_rms = lax.rsqrt(jnp.mean(value_entries * value_entries, axis=1, keepdims=True) + EPS)
    side = jnp.concatenate(parts_of(inverse_rms, 3) + [jnp.zeros((4, 125), BF16)], axis=1)
    message = jnp.concatenate(
        [
            inputs.reshape(4, 8, 1024),
            out_grad.reshape(4, 8, 1024),
            jnp.broadcast_to(side[:, None, :], (4, 8, 128)),
        ],
        axis=2,
    )
    message = jnp.broadcast_to(jnp.transpose(message, (1, 0, 2))[None], (HS, 8, 4, 2176))
    block = lax.all_to_all(
        message.reshape(16, 4, 2176), ("h", "z", "x"), split_axis=0, concat_axis=0, tiled=True
    )
    block = block.reshape(64, 2176)
    gain_block = lax.dynamic_slice(rms_gain_vector, (row * 1024,), (1024,))

    def normed_of(tokens):
        inverse = (
            tokens[:, 2048:2049].astype(F32)
            + tokens[:, 2049:2050].astype(F32)
            + tokens[:, 2050:2051].astype(F32)
        )
        estimate = tokens[:, :1024].astype(F32) * inverse
        return estimate, (estimate * gain_block).astype(BF16), tokens[:, 1024:2048]

    def partials(normed, grad):
        return jnp.concatenate(
            [
                product(normed, gate_weight),
                product(normed, up_weight),
                product_right_t(grad, down_weight),
            ],
            axis=1,
        ).reshape(4, 64, 3 * width)

    far_core, first = gather_half(lax.dynamic_slice(block, ((1 - z) * 32, 0), (32, 2176)), x)
    near_block, _ = lax.optimization_barrier(
        (lax.dynamic_slice(block, (z * 32, 0), (32, 2176)), first)
    )
    near_core, _ = gather_half(near_block, x)
    far_estimate, far_normed, far_grad = normed_of(both_cores(far_core))
    far = partials(far_normed, far_grad)
    near_core, far_own = lax.optimization_barrier((near_core, far[0]))
    near_estimate, near_normed, near_grad = normed_of(both_cores(near_core))
    near = partials(near_normed, near_grad)
    sums = sum_over_row(near, [far_own, far[1], far[2], far[3]])
    gate, up, hidden_grad = sums[:, :width], sums[:, width : 2 * width], sums[:, 2 * width :]
    sigma = jax.nn.sigmoid(gate)
    silu = gate * sigma
    units = jnp.concatenate(
        [
            (silu * up).astype(BF16),
            (hidden_grad * up * sigma * (1.0 + gate * (1.0 - sigma))).astype(BF16),
            (hidden_grad * silu).astype(BF16),
        ],
        axis=1,
    )
    units = gather_over_row(units)

    def backward(units):
        hidden, gate_grad, up_grad = units[:, :width], units[:, width : 2 * width], units[:, 2 * width :]
        grad = product_right_t(gate_grad, gate_weight) + product_right_t(up_grad, up_weight)
        return jnp.concatenate([product(hidden, down_weight), grad], axis=1)

    near_partial = backward(units[0])
    near_keep, _ = sum_over_core(near_partial, None)
    far_partial = backward(units[1])
    gain_partial = jnp.sum(near_partial[:, 1024:] * near_estimate, axis=0) + jnp.sum(
        far_partial[:, 1024:] * far_estimate, axis=0
    )
    far_keep, gain = sum_over_core(far_partial, gain_partial.reshape(8, 128))

    units = jnp.concatenate(units, axis=0)
    hidden, gate_grad, up_grad = units[:, :width], units[:, width : 2 * width], units[:, 2 * width :]
    normed = jnp.concatenate([near_normed, far_normed], axis=0)
    grad_full = jnp.concatenate([near_grad, far_grad], axis=0)
    down_weight_grad = product_left_t(hidden, grad_full).astype(BF16)
    far_keep, down_weight_grad = lax.optimization_barrier((far_keep, down_weight_grad))
    total, gain = sum_over_y(near_keep, far_keep, gain, x)
    normed, total = lax.optimization_barrier((normed, total))
    gate_weight_grad = product_left_t(normed, gate_grad).astype(BF16)
    up_weight_grad = product_left_t(normed, up_grad).astype(BF16)

    gain_parts = [p.reshape(4, 256) for p in parts_of(gain, 2)]
    gain_rows = jnp.broadcast_to(jnp.concatenate(gain_parts, axis=1)[None], (16, 4, 512))
    total = total.astype(BF16)
    total = jnp.where(z == 0, total, jnp.concatenate([total[32:], total[:32]], axis=0))
    message = jnp.concatenate([total.reshape(16, 4, 2048), gain_rows], axis=2)
    back = lax.all_to_all(message, ("h", "z", "x"), split_axis=0, concat_axis=0, tiled=True)
    back = back.reshape(HS, 8, 4, 2560).astype(F32)
    gain_grad = back[..., 2048:2304] + back[..., 2304:]
    gain_grad = (gain_grad[0] + gain_grad[1]).reshape(8192)
    back = back[0, :, :, :2048] + back[1, :, :, :2048]
    outputs = jnp.transpose(back[..., :1024].astype(BF16), (1, 0, 2)).reshape(4, 8192)
    normed_grad = jnp.transpose(back[..., 1024:], (1, 0, 2)).reshape(4, 8192)

    normalized = value_entries * inverse_rms
    scaled = normed_grad * rms_gain_vector
    input_gradient = inverse_rms * (
        scaled - normalized * jnp.mean(scaled * normalized, axis=1, keepdims=True)
    )
    return (
        outputs,
        input_gradient.astype(BF16),
        gain_grad,
        gate_weight_grad,
        up_weight_grad,
        down_weight_grad,
    )


def solution(mesh):
    fine = Mesh(mesh.devices.reshape(ZS, XS, HS, YS, CS), AXES)
    row, col = AXES[:2], AXES[2:]
    in_specs = (P(AXES, None), P(), P(row, col), P(row, col), P(col, row), P(AXES, None))
    out_specs = (P(AXES, None), P(AXES, None), P(), P(row, col), P(row, col), P(col, row))
    return jax.shard_map(
        per_device, mesh=fine, in_specs=in_specs, out_specs=out_specs, check_vma=False
    )
```

```python
import math

import jax
import jax.numpy as jnp
from jax import lax
from jax.experimental import pallas as pl
from jax.experimental.pallas import tpu as pltpu
from jax.sharding import Mesh, PartitionSpec as P

EPS = 1e-05
F32 = jnp.float32
BF16 = jnp.bfloat16
ZS, XS, HS, YS, CS = 2, 4, 2, 4, 2
AXES = ("z", "x", "h", "y", "core")


def send(value, z=0, x=0, h=0, y=0, c=0):
    pairs = []
    for z0 in range(ZS):
        for x0 in range(XS):
            for h0 in range(HS):
                for y0 in range(YS):
                    for c0 in range(CS):
                        source = (((z0 * XS + x0) * HS + h0) * YS + y0) * CS + c0
                        z1, x1, h1 = (z0 + z) % ZS, (x0 + x) % XS, (h0 + h) % HS
                        y1, c1 = (y0 + y) % YS, (c0 + c) % CS
                        pairs.append((source, (((z1 * XS + x1) * HS + h1) * YS + y1) * CS + c1))
    return lax.ppermute(value, AXES, pairs)


def contract(left, right, dims):
    return lax.dot_general(left, right, ((dims[:1], dims[1:]), ((), ())), preferred_element_type=F32)


def rounded(value):
    return lax.reduce_precision(value, 8, 7)


def parts_of(value, count):
    parts = []
    for _ in range(count):
        top = rounded(value)
        parts.append(top.astype(BF16))
        value = value - top
    return parts


def gather_half(own, x):
    n = own.shape[1]
    over_y = {0: own}
    for dy in (1, 3, 2):
        over_y[-dy % YS] = send(own, y=dy)
    core = jnp.zeros((128, n), own.dtype)
    for dy in range(YS):
        core = lax.dynamic_update_slice(core, over_y[dy], ((dy - x) % XS * 32, 0))
    return core, over_y[3]


TILE = 256


def call(kernel, grid, arrays, specs, outs, flops, scratch=()):
    size = sum(array.size * array.dtype.itemsize for array in arrays)
    size += sum(math.prod(shape) * jnp.dtype(dtype).itemsize for shape, dtype, _ in outs)
    return pl.pallas_call(
        kernel,
        grid=grid,
        in_specs=specs,
        out_specs=[spec for _, _, spec in outs],
        out_shape=[jax.ShapeDtypeStruct(shape, dtype) for shape, dtype, _ in outs],
        scratch_shapes=scratch,
        compiler_params=pltpu.CompilerParams(vmem_limit_bytes=28 * 1024 * 1024),
        cost_estimate=pl.CostEstimate(flops=flops, bytes_accessed=size, transcendentals=0),
    )(*arrays)


def whole(rows, columns):
    return pl.BlockSpec((rows, columns), lambda j: (0, 0))


def columns_at(rows, columns=3 * TILE):
    return pl.BlockSpec((rows, columns), lambda j: (0, j))


def weight_specs():
    return [columns_at(1024, TILE), columns_at(1024, TILE), pl.BlockSpec((TILE, 1024), lambda j: (j, 0))]


def estimates(core_ref, other_ref):
    for i in range(XS):
        for k, ref in enumerate((core_ref, other_ref)):
            rows = ref[i * 32 : i * 32 + 32, :]
            side = rows[:, 2048:].astype(F32)
            inverse = side[:, 0:1] + side[:, 1:2] + side[:, 2:3]
            yield i * 64 + k * 32, rows[:, :1024].astype(F32) * inverse, rows[:, 1024:2048]


def multiply_half(core, other, gain_block, weights, pieces):
    def kernel(core_ref, other_ref, gain_ref, gate_ref, up_ref, down_ref, normed, grad, *refs):
        @pl.when(pl.program_id(0) == 0)
        def _():
            for at, estimate, rows in estimates(core_ref, other_ref):
                normed[at : at + 32, :] = (estimate * gain_ref[...]).astype(BF16)
                grad[at : at + 32, :] = rows

        sums = (
            contract(normed[...], gate_ref[...], (1, 0)),
            contract(normed[...], up_ref[...], (1, 0)),
            contract(grad[...], down_ref[...], (1, 1)),
        )
        for (first, count, dtype), ref in zip(pieces, refs, strict=True):
            for k, value in enumerate(sums):
                ref[:, k * TILE : k * TILE + TILE] = value[first : first + count].astype(dtype)

    width = weights[0].shape[1]
    outs = [((256, 1024), BF16, whole(256, 1024))] * 2
    outs += [((rows, 3 * width), dtype, columns_at(rows)) for _, rows, dtype in pieces]
    specs = [whole(128, 2176), whole(128, 2176), whole(1, 1024)] + weight_specs()
    flops = 6 * 256 * 1024 * width
    return call(kernel, (width // TILE,), [core, other, gain_block, *weights], specs, outs, flops)


def finish_sums(near, q, top1, bottom1, top2, bottom2):
    def kernel(near_ref, q_ref, top1_ref, bottom1_ref, top2_ref, bottom2_ref, out_ref):
        for rows, one, two in (
            (slice(0, 32), top1_ref, top2_ref),
            (slice(32, 64), bottom1_ref, bottom2_ref),
        ):
            total = near_ref[rows, :] + q_ref[rows, :].astype(F32)
            total = total + one[...].astype(F32) + two[...].astype(F32)
            gate, up, grad = (total[:, k * TILE : k * TILE + TILE] for k in range(3))
            sigma = jax.nn.sigmoid(gate)
            silu = gate * sigma
            out_ref[rows, :TILE] = (silu * up).astype(BF16)
            gate_grad = grad * up * sigma * (1.0 + gate * (1.0 - sigma))
            out_ref[rows, TILE : 2 * TILE] = gate_grad.astype(BF16)
            out_ref[rows, 2 * TILE :] = (grad * silu).astype(BF16)

    width = near.shape[1]
    specs = [columns_at(64)] * 2 + [columns_at(32)] * 4
    outs = [((64, width), BF16, columns_at(64))]
    arrays = [near, q, top1, bottom1, top2, bottom2]
    return call(kernel, (width // (3 * TILE),), arrays, specs, outs, 64 * width * 8)[0]


def multiply_back(units, core, other, weights, gain_before):
    last = weights[0].shape[1] // TILE - 1
    with_before = gain_before is not None

    def kernel(*refs):
        unit_refs, refs = refs[:4], refs[4:]
        gate_ref, up_ref, down_ref, core_ref, other_ref, *refs = refs
        before_ref, refs = (refs[0], refs[1:]) if with_before else (None, refs)
        keep_ref, give_ref, gain_ref, out_sum, grad_sum = refs
        j = pl.program_id(0)

        @pl.when(j == 0)
        def _():
            out_sum[...] = jnp.zeros_like(out_sum)
            grad_sum[...] = jnp.zeros_like(grad_sum)

        unit = jnp.concatenate([ref[...] for ref in unit_refs], axis=0)
        out_sum[...] += contract(unit[:, :TILE], down_ref[...], (1, 0))
        grad_sum[...] += contract(unit[:, TILE : 2 * TILE], gate_ref[...], (1, 1)) + contract(
            unit[:, 2 * TILE :], up_ref[...], (1, 1)
        )

        @pl.when(j == last)
        def _():
            gain = before_ref[0:1, :] if with_before else jnp.zeros((1, 1024), F32)
            for at, estimate, _ in estimates(core_ref, other_ref):
                grad = grad_sum[at : at + 32, :]
                gain = gain + jnp.sum(grad * estimate, axis=0, keepdims=True)
                ref = give_ref if at // 32 % 2 else keep_ref
                to = at // 64 * 32
                ref[to : to + 32, :1024] = out_sum[at : at + 32, :]
                ref[to : to + 32, 1024:] = grad
            gain_ref[...] = jnp.broadcast_to(gain, (8, 1024))
            if with_before:
                give_ref[128:136, :1024] = jnp.broadcast_to(gain, (8, 1024))
                give_ref[128:136, 1024:] = jnp.broadcast_to(gain, (8, 1024))

    width = weights[0].shape[1]
    give = 136 if with_before else 128
    arrays = [*units, *weights, core, other] + ([gain_before] if with_before else [])
    specs = [columns_at(64)] * 4 + weight_specs() + [whole(128, 2176)] * 2
    specs += [whole(8, 1024)] if with_before else []
    outs = [((rows, 2048), F32, whole(rows, 2048)) for rows in (128, give)]
    outs += [((8, 1024), F32, whole(8, 1024))]
    scratch = [pltpu.VMEM((256, 1024), F32)] * 2
    flops = 6 * 256 * 1024 * width
    return call(kernel, (width // TILE,), arrays, specs, outs, flops, scratch)


def weight_grad(units, parts, sides, left):
    width = units[0].shape[1] // 3
    count = len(parts)

    def kernel(*refs):
        side = jnp.concatenate([ref[...] for ref in refs[8 * count : 8 * count + 2]], axis=0)
        for k in range(count):
            unit = jnp.concatenate([ref[...] for ref in refs[8 * k : 8 * k + 8]], axis=0)
            pair = (unit, side) if left else (side, unit)
            refs[8 * count + 2 + k][...] = contract(*pair, (0, 0)).astype(BF16)

    specs = [
        pl.BlockSpec((64, TILE), lambda j, part=part: (0, 3 * j + part))
        for part in parts
        for _ in units
    ]
    specs += [whole(256, 1024)] * 2
    if left:
        out = ((width, 1024), BF16, pl.BlockSpec((TILE, 1024), lambda j: (j, 0)))
    else:
        out = ((1024, width), BF16, columns_at(1024, TILE))
    arrays = [*units] * count + list(sides)
    flops = 2 * 512 * 1024 * width * count
    return call(kernel, (width // TILE,), arrays, specs, [out] * count, flops)


def sum_over_y(near, far, gain, x):
    n = near.shape[1]

    def piece(dy):
        start = (dy - x) % XS * 32
        halves = [lax.dynamic_slice(half, (start, 0), (32, n)) for half in (near, far)]
        return jnp.concatenate(halves, axis=0)

    def gain_of(parts):
        return parts[:8].astype(F32) + parts[8:16].astype(F32)

    parts = jnp.concatenate(parts_of(gain, 2) + [jnp.zeros((48, 128), BF16)], axis=0)
    gains = {0: gain_of(parts)}
    total = piece(0)
    for dy in (1, 3, 2):
        got = send(jnp.concatenate([piece(dy).astype(BF16), parts], axis=1), y=dy)
        total = total + got[:, :n].astype(F32)
        gains[dy] = gain_of(got[:, n:])
    return total, (gains[0] + gains[2]) + (gains[1] + gains[3])


def sum_over_row(far, near):
    own, to1, to2, to3 = far
    near0, near1_top, near1_bottom, near2, near3_top, near3_bottom = near
    m12 = send(to2, z=1).astype(F32)
    m11 = send(to1, x=1).astype(F32)
    m13 = send(to3, x=3).astype(F32)
    first1 = send(near1_bottom, x=1)
    first2 = send(near3_top, x=3)
    n1 = send((near2[:32] + m12[:32]).astype(BF16), x=1).astype(F32)
    n2 = send((near2[32:] + m12[32:]).astype(BF16), x=3).astype(F32)
    q = send((own + m11 + m13).astype(BF16), z=1)
    last1 = (near1_top + n1).astype(BF16)
    last2 = (near3_bottom + n2).astype(BF16)
    last1, last2, first1, first2 = lax.optimization_barrier((last1, last2, first1, first2))
    return finish_sums(near0, q, send(last1, x=1), first1, first2, send(last2, x=3))


def gather_over_row(own):
    h = own.shape[0] // 2
    a = send(own, x=1)
    b = send(own, x=3)
    p = send(own, z=1)
    a2 = send(a[:h], x=1)
    b2 = send(b[h:], x=3)
    pa = send(p, x=1)
    pb = send(p, x=3)
    across = jnp.concatenate([a2, b2], axis=0)
    p2 = send(across, z=1)
    return [own, b, across, a], [p, pb, p2, pa]


def per_device(inputs, rms_gain_vector, gate_weight, up_weight, down_weight, out_grad):
    z, x = lax.axis_index("z"), lax.axis_index("x")
    row = z * XS + x

    value_entries = inputs.astype(F32)
    inverse_rms = lax.rsqrt(jnp.mean(value_entries * value_entries, axis=1, keepdims=True) + EPS)
    side = jnp.concatenate(parts_of(inverse_rms, 3) + [jnp.zeros((4, 125), BF16)], axis=1)
    message = jnp.concatenate(
        [
            inputs.reshape(4, 8, 1024),
            out_grad.reshape(4, 8, 1024),
            jnp.broadcast_to(side[:, None, :], (4, 8, 128)),
        ],
        axis=2,
    )
    message = jnp.broadcast_to(jnp.transpose(message, (1, 0, 2))[None], (HS, 8, 4, 2176))
    block = lax.all_to_all(
        message.reshape(16, 4, 2176), ("h", "z", "x"), split_axis=0, concat_axis=0, tiled=True
    )
    block = block.reshape(64, 2176)
    gain_block = lax.dynamic_slice(rms_gain_vector, (row * 1024,), (1024,))

    gain_block = gain_block.reshape(1, 1024)
    weights = (gate_weight, up_weight, down_weight)

    far_core, first = gather_half(lax.dynamic_slice(block, ((1 - z) * 32, 0), (32, 2176)), x)
    near_block, _ = lax.optimization_barrier(
        (lax.dynamic_slice(block, (z * 32, 0), (32, 2176)), first)
    )
    near_core, _ = gather_half(near_block, x)
    far_tokens = (far_core, send(far_core, c=1))
    far_normed, far_grad, far_own, *far = multiply_half(
        *far_tokens,
        gain_block,
        weights,
        [(0, 64, F32), (64, 64, BF16), (128, 64, BF16), (192, 64, BF16)],
    )
    near_core, far_own = lax.optimization_barrier((near_core, far_own))
    near_tokens = (near_core, send(near_core, c=1))
    near_normed, near_grad, *near = multiply_half(
        *near_tokens,
        gain_block,
        weights,
        [
            (0, 64, F32),
            (64, 32, F32),
            (96, 32, BF16),
            (128, 64, F32),
            (192, 32, BF16),
            (224, 32, F32),
        ],
    )
    near_units, far_units = gather_over_row(sum_over_row([far_own, *far], near))

    near_keep, near_give, gain = multiply_back(near_units, *near_tokens, weights, None)
    near_keep = near_keep + send(near_give, c=1)
    far_keep, far_give, gain = multiply_back(far_units, *far_tokens, weights, gain)
    taken = send(far_give, c=1)
    far_keep = far_keep + taken[:128]
    gain = (gain[0] + taken[128, :1024]).reshape(8, 128)

    units = near_units + far_units
    (down_weight_grad,) = weight_grad(units, (0,), (near_grad, far_grad), True)
    far_keep, down_weight_grad = lax.optimization_barrier((far_keep, down_weight_grad))
    total, gain = sum_over_y(near_keep, far_keep, gain, x)
    near_normed, total = lax.optimization_barrier((near_normed, total))
    gate_weight_grad, up_weight_grad = weight_grad(
        units, (1, 2), (near_normed, far_normed), False
    )

    gain_parts = [p.reshape(4, 256) for p in parts_of(gain, 2)]
    gain_rows = jnp.broadcast_to(jnp.concatenate(gain_parts, axis=1)[None], (16, 4, 512))
    total = total.astype(BF16)
    total = jnp.where(z == 0, total, jnp.concatenate([total[32:], total[:32]], axis=0))
    message = jnp.concatenate([total.reshape(16, 4, 2048), gain_rows], axis=2)
    back = lax.all_to_all(message, ("h", "z", "x"), split_axis=0, concat_axis=0, tiled=True)
    back = back.reshape(HS, 8, 4, 2560).astype(F32)
    gain_grad = back[..., 2048:2304] + back[..., 2304:]
    gain_grad = (gain_grad[0] + gain_grad[1]).reshape(8192)
    back = back[0, :, :, :2048] + back[1, :, :, :2048]
    outputs = jnp.transpose(back[..., :1024].astype(BF16), (1, 0, 2)).reshape(4, 8192)
    normed_grad = jnp.transpose(back[..., 1024:], (1, 0, 2)).reshape(4, 8192)

    normalized = value_entries * inverse_rms
    scaled = normed_grad * rms_gain_vector
    input_gradient = inverse_rms * (
        scaled - normalized * jnp.mean(scaled * normalized, axis=1, keepdims=True)
    )
    return (
        outputs,
        input_gradient.astype(BF16),
        gain_grad,
        gate_weight_grad,
        up_weight_grad,
        down_weight_grad,
    )


def solution(mesh):
    fine = Mesh(mesh.devices.reshape(ZS, XS, HS, YS, CS), AXES)
    row, col = AXES[:2], AXES[2:]
    in_specs = (P(AXES, None), P(), P(row, col), P(row, col), P(col, row), P(AXES, None))
    out_specs = (P(AXES, None), P(AXES, None), P(), P(row, col), P(row, col), P(col, row))
    return jax.shard_map(
        per_device, mesh=fine, in_specs=in_specs, out_specs=out_specs, check_vma=False
    )
```

```python
import jax
import jax.numpy as jnp
from jax import lax
from jax.sharding import Mesh, PartitionSpec as P

EPS = 1e-05
F32 = jnp.float32
BF16 = jnp.bfloat16
ZS, XS, HS, YS, CS = 2, 4, 2, 4, 2
AXES = ("z", "x", "h", "y", "core")


def send(value, z=0, x=0, h=0, y=0, c=0):
    pairs = []
    for z0 in range(ZS):
        for x0 in range(XS):
            for h0 in range(HS):
                for y0 in range(YS):
                    for c0 in range(CS):
                        source = (((z0 * XS + x0) * HS + h0) * YS + y0) * CS + c0
                        z1, x1, h1 = (z0 + z) % ZS, (x0 + x) % XS, (h0 + h) % HS
                        y1, c1 = (y0 + y) % YS, (c0 + c) % CS
                        pairs.append((source, (((z1 * XS + x1) * HS + h1) * YS + y1) * CS + c1))
    return lax.ppermute(value, AXES, pairs)


def product(left, right):
    return jnp.dot(left, right, preferred_element_type=F32)


def product_right_t(left, right):
    return lax.dot_general(left, right, (((1,), (1,)), ((), ())), preferred_element_type=F32)


def product_left_t(left, right):
    return lax.dot_general(left, right, (((0,), (0,)), ((), ())), preferred_element_type=F32)


def rounded(value):
    return lax.reduce_precision(value, 8, 7)


def parts_of(value, count):
    parts = []
    for _ in range(count):
        top = rounded(value)
        parts.append(top.astype(BF16))
        value = value - top
    return parts


def gather_half(own, x):
    n = own.shape[1]
    over_y = {0: own}
    for dy in (1, 3, 2):
        over_y[-dy % YS] = send(own, y=dy)
    core = jnp.zeros((128, n), own.dtype)
    for dy in range(YS):
        core = lax.dynamic_update_slice(core, over_y[dy], ((dy - x) % XS * 32, 0))
    return core, over_y[3]


def both_cores(core):
    return jnp.concatenate([core, send(core, c=1)], axis=0)


def by_core(blocks):
    return jnp.concatenate([b[:32] for b in blocks] + [b[32:] for b in blocks], axis=0)


def sum_over_core(partial, gain_partial):
    give = partial[128:]
    if gain_partial is not None:
        gain_rows = jnp.pad(gain_partial, ((0, 0), (0, partial.shape[1] - 128)))
        give = jnp.concatenate([give, gain_rows], axis=0)
    taken = send(give, c=1)
    if gain_partial is not None:
        gain_partial = gain_partial + taken[128:, :128]
    return partial[:128] + taken[:128], gain_partial


def sum_over_y(near, far, gain, x):
    n = near.shape[1]

    def piece(dy):
        start = (dy - x) % XS * 32
        halves = [lax.dynamic_slice(half, (start, 0), (32, n)) for half in (near, far)]
        return jnp.concatenate(halves, axis=0)

    def gain_of(parts):
        return parts[:8].astype(F32) + parts[8:16].astype(F32)

    parts = jnp.concatenate(parts_of(gain, 2) + [jnp.zeros((48, 128), BF16)], axis=0)
    gains = {0: gain_of(parts)}
    total = piece(0)
    for dy in (1, 3, 2):
        got = send(jnp.concatenate([piece(dy).astype(BF16), parts], axis=1), y=dy)
        total = total + got[:, :n].astype(F32)
        gains[dy] = gain_of(got[:, n:])
    return total, (gains[0] + gains[2]) + (gains[1] + gains[3])


def sum_over_row(far, near):
    own, to1, to2, to3 = far
    near0, near1_top, near1_bottom, near2, near3_top, near3_bottom = near
    m12 = send(to2, z=1).astype(F32)
    m11 = send(to1, x=1).astype(F32)
    m13 = send(to3, x=3).astype(F32)
    first1 = send(near1_bottom, x=1)
    first2 = send(near3_top, x=3)
    n1 = send((near2[:32] + m12[:32]).astype(BF16), x=1).astype(F32)
    n2 = send((near2[32:] + m12[32:]).astype(BF16), x=3).astype(F32)
    q = send((own + m11 + m13).astype(BF16), z=1)
    last1 = (near1_top + n1).astype(BF16)
    last2 = (near3_bottom + n2).astype(BF16)
    last1, last2, first1, first2 = lax.optimization_barrier((last1, last2, first1, first2))
    one = jnp.concatenate([send(last1, x=1), first1], axis=0).astype(F32)
    two = jnp.concatenate([first2, send(last2, x=3)], axis=0).astype(F32)
    return near0 + q.astype(F32) + one + two


def gather_over_row(own):
    h = own.shape[0] // 2
    a = send(own, x=1)
    b = send(own, x=3)
    p = send(own, z=1)
    a2 = send(a[:h], x=1)
    b2 = send(b[h:], x=3)
    pa = send(p, x=1)
    pb = send(p, x=3)
    across = jnp.concatenate([a2, b2], axis=0)
    p2 = send(across, z=1)
    return [own, b, across, a], [p, pb, p2, pa]


def per_device(inputs, rms_gain_vector, gate_weight, up_weight, down_weight, out_grad):
    z, x = lax.axis_index("z"), lax.axis_index("x")
    row = z * XS + x
    width = gate_weight.shape[1]

    value_entries = inputs.astype(F32)
    inverse_rms = lax.rsqrt(jnp.mean(value_entries * value_entries, axis=1, keepdims=True) + EPS)
    side = jnp.concatenate(parts_of(inverse_rms, 3) + [jnp.zeros((4, 125), BF16)], axis=1)
    message = jnp.concatenate(
        [
            inputs.reshape(4, 8, 1024),
            out_grad.reshape(4, 8, 1024),
            jnp.broadcast_to(side[:, None, :], (4, 8, 128)),
        ],
        axis=2,
    )
    message = jnp.broadcast_to(jnp.transpose(message, (1, 0, 2))[None], (HS, 8, 4, 2176))
    block = lax.all_to_all(
        message.reshape(16, 4, 2176), ("h", "z", "x"), split_axis=0, concat_axis=0, tiled=True
    )
    block = block.reshape(64, 2176)
    gain_block = lax.dynamic_slice(rms_gain_vector, (row * 1024,), (1024,))

    def normed_of(tokens):
        inverse = (
            tokens[:, 2048:2049].astype(F32)
            + tokens[:, 2049:2050].astype(F32)
            + tokens[:, 2050:2051].astype(F32)
        )
        estimate = tokens[:, :1024].astype(F32) * inverse
        return estimate, (estimate * gain_block).astype(BF16), tokens[:, 1024:2048]

    def partials(normed, grad):
        sums = [
            product(normed, gate_weight),
            product(normed, up_weight),
            product_right_t(grad, down_weight),
        ]

        def block(dx, dtype, cores=(0, 1)):
            rows = [
                jnp.concatenate([value[c * 128 + dx * 32 :][:32] for value in sums], axis=1)
                for c in cores
            ]
            return jnp.concatenate(rows, axis=0).astype(dtype)

        return block

    far_core, first = gather_half(lax.dynamic_slice(block, ((1 - z) * 32, 0), (32, 2176)), x)
    near_block, _ = lax.optimization_barrier(
        (lax.dynamic_slice(block, (z * 32, 0), (32, 2176)), first)
    )
    near_core, _ = gather_half(near_block, x)
    far_estimate, far_normed, far_grad = normed_of(both_cores(far_core))
    far = partials(far_normed, far_grad)
    far = [far(0, F32), far(1, BF16), far(2, BF16), far(3, BF16)]
    near_core, far[0] = lax.optimization_barrier((near_core, far[0]))
    near_estimate, near_normed, near_grad = normed_of(both_cores(near_core))
    near = partials(near_normed, near_grad)
    near = [
        near(0, F32),
        near(1, F32, (0,)),
        near(1, BF16, (1,)),
        near(2, F32),
        near(3, BF16, (0,)),
        near(3, F32, (1,)),
    ]
    sums = sum_over_row(far, near)
    gate, up, hidden_grad = sums[:, :width], sums[:, width : 2 * width], sums[:, 2 * width :]
    sigma = jax.nn.sigmoid(gate)
    silu = gate * sigma
    units = jnp.concatenate(
        [
            (silu * up).astype(BF16),
            (hidden_grad * up * sigma * (1.0 + gate * (1.0 - sigma))).astype(BF16),
            (hidden_grad * silu).astype(BF16),
        ],
        axis=1,
    )
    near_units, far_units = gather_over_row(units)
    near_units = by_core(lax.optimization_barrier(near_units))
    far_units = by_core(lax.optimization_barrier(far_units))

    def backward(units):
        hidden, gate_grad, up_grad = units[:, :width], units[:, width : 2 * width], units[:, 2 * width :]
        grad = product_right_t(gate_grad, gate_weight) + product_right_t(up_grad, up_weight)
        return jnp.concatenate([product(hidden, down_weight), grad], axis=1)

    near_partial = backward(near_units)
    near_keep, _ = sum_over_core(near_partial, None)
    far_partial = backward(far_units)
    gain_partial = jnp.sum(near_partial[:, 1024:] * near_estimate, axis=0) + jnp.sum(
        far_partial[:, 1024:] * far_estimate, axis=0
    )
    far_keep, gain = sum_over_core(far_partial, gain_partial.reshape(8, 128))

    *late, far_keep = lax.optimization_barrier((near_units, far_units, far_keep))

    def of_all(part):
        return jnp.concatenate(
            [unit[:, part * width : (part + 1) * width] for unit in late], axis=0
        )

    grad_full = jnp.concatenate([near_grad, far_grad], axis=0)
    down_weight_grad = product_left_t(of_all(0), grad_full).astype(BF16)
    total, gain = sum_over_y(near_keep, far_keep, gain, x)
    normed, total, down_weight_grad = lax.optimization_barrier(
        (jnp.concatenate([near_normed, far_normed], axis=0), total, down_weight_grad)
    )
    gate_weight_grad = product_left_t(normed, of_all(1)).astype(BF16)
    up_weight_grad = product_left_t(normed, of_all(2)).astype(BF16)

    gain_parts = [p.reshape(4, 256) for p in parts_of(gain, 2)]
    gain_rows = jnp.broadcast_to(jnp.concatenate(gain_parts, axis=1)[None], (16, 4, 512))
    total = total.astype(BF16)
    total = jnp.where(z == 0, total, jnp.concatenate([total[32:], total[:32]], axis=0))
    message = jnp.concatenate([total.reshape(16, 4, 2048), gain_rows], axis=2)
    back = lax.all_to_all(message, ("h", "z", "x"), split_axis=0, concat_axis=0, tiled=True)
    back = back.reshape(HS, 8, 4, 2560).astype(F32)
    gain_grad = back[..., 2048:2304] + back[..., 2304:]
    gain_grad = (gain_grad[0] + gain_grad[1]).reshape(8192)
    back = back[0, :, :, :2048] + back[1, :, :, :2048]
    outputs = jnp.transpose(back[..., :1024].astype(BF16), (1, 0, 2)).reshape(4, 8192)
    normed_grad = jnp.transpose(back[..., 1024:], (1, 0, 2)).reshape(4, 8192)

    normalized = value_entries * inverse_rms
    scaled = normed_grad * rms_gain_vector
    input_gradient = inverse_rms * (
        scaled - normalized * jnp.mean(scaled * normalized, axis=1, keepdims=True)
    )
    return (
        outputs,
        input_gradient.astype(BF16),
        gain_grad,
        gate_weight_grad,
        up_weight_grad,
        down_weight_grad,
    )


def solution(mesh):
    fine = Mesh(mesh.devices.reshape(ZS, XS, HS, YS, CS), AXES)
    row, col = AXES[:2], AXES[2:]
    in_specs = (P(AXES, None), P(), P(row, col), P(row, col), P(col, row), P(AXES, None))
    out_specs = (P(AXES, None), P(AXES, None), P(), P(row, col), P(row, col), P(col, row))
    return jax.shard_map(
        per_device, mesh=fine, in_specs=in_specs, out_specs=out_specs, check_vma=False
    )
```

```python
import jax
import jax.numpy as jnp
from jax import lax
from jax.sharding import Mesh, PartitionSpec as P

EPS = 1e-05
F32 = jnp.float32
BF16 = jnp.bfloat16
ZS, XS, HS, YS, CS = 2, 4, 2, 4, 2
AXES = ("z", "x", "h", "y", "core")


def send(value, z=0, x=0, h=0, y=0, c=0):
    pairs = []
    for z0 in range(ZS):
        for x0 in range(XS):
            for h0 in range(HS):
                for y0 in range(YS):
                    for c0 in range(CS):
                        source = (((z0 * XS + x0) * HS + h0) * YS + y0) * CS + c0
                        z1, x1, h1 = (z0 + z) % ZS, (x0 + x) % XS, (h0 + h) % HS
                        y1, c1 = (y0 + y) % YS, (c0 + c) % CS
                        pairs.append((source, (((z1 * XS + x1) * HS + h1) * YS + y1) * CS + c1))
    return lax.ppermute(value, AXES, pairs)


def product(left, right):
    return jnp.dot(left, right, preferred_element_type=F32)


def product_right_t(left, right):
    return lax.dot_general(left, right, (((1,), (1,)), ((), ())), preferred_element_type=F32)


def product_left_t(left, right):
    return lax.dot_general(left, right, (((0,), (0,)), ((), ())), preferred_element_type=F32)


def rounded(value):
    return lax.reduce_precision(value, 8, 7)


def parts_of(value, count):
    parts = []
    for _ in range(count):
        top = rounded(value)
        parts.append(top.astype(BF16))
        value = value - top
    return parts


def gather_half(own, x):
    n = own.shape[1]
    over_y = {0: own}
    for dy in (1, 3, 2):
        over_y[-dy % YS] = send(own, y=dy)
    core = jnp.zeros((128, n), own.dtype)
    for dy in range(YS):
        core = lax.dynamic_update_slice(core, over_y[dy], ((dy - x) % XS * 32, 0))
    return core, over_y[3]


def both_cores(core):
    return jnp.concatenate([core, send(core, c=1)], axis=0)


def by_core(blocks):
    return jnp.concatenate([b[:32] for b in blocks] + [b[32:] for b in blocks], axis=0)


def gain_of(parts):
    return parts[:8].astype(F32) + parts[8:16].astype(F32)


def sum_over_core(partial, gain_partial):
    give = partial[128:].astype(BF16)
    if gain_partial is not None:
        gain_rows = jnp.concatenate(parts_of(gain_partial, 2), axis=0)
        padded = jnp.pad(gain_rows, ((0, 0), (0, partial.shape[1] - 128)))
        give = jnp.concatenate([give, padded], axis=0)
    taken = send(give, c=1)
    if gain_partial is not None:
        gain_partial = gain_of(gain_rows) + gain_of(taken[128:, :128])
    return partial[:128] + taken[:128].astype(F32), gain_partial


def sum_over_y(near, far, gain, x):
    n = near.shape[1]

    def piece(dy):
        start = (dy - x) % XS * 32
        halves = [lax.dynamic_slice(half, (start, 0), (32, n)) for half in (near, far)]
        return jnp.concatenate(halves, axis=0)

    parts = jnp.concatenate(parts_of(gain, 2) + [jnp.zeros((48, 128), BF16)], axis=0)
    gains = {0: gain_of(parts)}
    total = piece(0)
    for dy in (1, 3, 2):
        got = send(jnp.concatenate([piece(dy).astype(BF16), parts], axis=1), y=dy)
        total = total + got[:, :n].astype(F32)
        gains[dy] = gain_of(got[:, n:])
    return total, (gains[0] + gains[2]) + (gains[1] + gains[3])


def sum_over_row(far, near):
    own, to1, to2, to3 = far
    near0, near1_top, near1_bottom, near2, near3_top, near3_bottom = near
    m12 = send(to2, z=1).astype(F32)
    m11 = send(to1, x=1).astype(F32)
    m13 = send(to3, x=3).astype(F32)
    first1 = send(near1_bottom, x=1)
    first2 = send(near3_top, x=3)
    n1 = send((near2[:32] + m12[:32]).astype(BF16), x=1).astype(F32)
    n2 = send((near2[32:] + m12[32:]).astype(BF16), x=3).astype(F32)
    q = send((own.astype(F32) + m11 + m13).astype(BF16), z=1)
    last1 = (near1_top + n1).astype(BF16)
    last2 = (near3_bottom + n2).astype(BF16)
    last1, last2, first1, first2 = lax.optimization_barrier((last1, last2, first1, first2))
    one = jnp.concatenate([send(last1, x=1), first1], axis=0).astype(F32)
    two = jnp.concatenate([first2, send(last2, x=3)], axis=0).astype(F32)
    return near0 + q.astype(F32) + one + two


def gather_over_row(own):
    h = own.shape[0] // 2
    a = send(own, x=1)
    b = send(own, x=3)
    p = send(own, z=1)
    a2 = send(a[:h], x=1)
    b2 = send(b[h:], x=3)
    pa = send(p, x=1)
    pb = send(p, x=3)
    across = jnp.concatenate([a2, b2], axis=0)
    p2 = send(across, z=1)
    return [own, b, across, a], [p, pb, p2, pa]


def per_device(inputs, rms_gain_vector, gate_weight, up_weight, down_weight, out_grad):
    z, x = lax.axis_index("z"), lax.axis_index("x")
    row = z * XS + x
    width = gate_weight.shape[1]

    value_entries = inputs.astype(F32)
    inverse_rms = lax.rsqrt(jnp.mean(value_entries * value_entries, axis=1, keepdims=True) + EPS)
    side = jnp.concatenate(parts_of(inverse_rms, 3) + [jnp.zeros((4, 125), BF16)], axis=1)
    message = jnp.concatenate(
        [
            inputs.reshape(4, 8, 1024),
            out_grad.reshape(4, 8, 1024),
            jnp.broadcast_to(side[:, None, :], (4, 8, 128)),
        ],
        axis=2,
    )
    message = jnp.broadcast_to(jnp.transpose(message, (1, 0, 2))[None], (HS, 8, 4, 2176))
    block = lax.all_to_all(
        message.reshape(16, 4, 2176), ("h", "z", "x"), split_axis=0, concat_axis=0, tiled=True
    )
    block = block.reshape(64, 2176)
    gain_block = lax.dynamic_slice(rms_gain_vector, (row * 1024,), (1024,))

    def normed_of(tokens):
        inverse = (
            tokens[:, 2048:2049].astype(F32)
            + tokens[:, 2049:2050].astype(F32)
            + tokens[:, 2050:2051].astype(F32)
        )
        estimate = tokens[:, :1024].astype(F32) * inverse
        return estimate, (estimate * gain_block).astype(BF16), tokens[:, 1024:2048]

    def partials(normed, grad):
        sums = [
            product(normed, gate_weight),
            product(normed, up_weight),
            product_right_t(grad, down_weight),
        ]

        def block(dx, dtype, cores=(0, 1)):
            rows = [
                jnp.concatenate([value[c * 128 + dx * 32 :][:32] for value in sums], axis=1)
                for c in cores
            ]
            return jnp.concatenate(rows, axis=0).astype(dtype)

        return block

    far_core, first = gather_half(lax.dynamic_slice(block, ((1 - z) * 32, 0), (32, 2176)), x)
    near_block, _ = lax.optimization_barrier(
        (lax.dynamic_slice(block, (z * 32, 0), (32, 2176)), first)
    )
    near_core, _ = gather_half(near_block, x)
    far_estimate, far_normed, far_grad = normed_of(both_cores(far_core))
    far = partials(far_normed, far_grad)
    far = [far(0, BF16), far(1, BF16), far(2, BF16), far(3, BF16)]
    near_core, far[0] = lax.optimization_barrier((near_core, far[0]))
    near_estimate, near_normed, near_grad = normed_of(both_cores(near_core))
    near = partials(near_normed, near_grad)
    near = [
        near(0, F32),
        near(1, F32, (0,)),
        near(1, BF16, (1,)),
        near(2, F32),
        near(3, BF16, (0,)),
        near(3, F32, (1,)),
    ]
    sums = sum_over_row(far, near)
    normed = jnp.concatenate([near_normed, far_normed], axis=0)
    grad_full = jnp.concatenate([near_grad, far_grad], axis=0)
    normed, grad_full, sums = lax.optimization_barrier((normed, grad_full, sums))
    gate, up, hidden_grad = sums[:, :width], sums[:, width : 2 * width], sums[:, 2 * width :]
    sigma = jax.nn.sigmoid(gate)
    silu = gate * sigma
    units = jnp.concatenate(
        [
            (silu * up).astype(BF16),
            (hidden_grad * up * sigma * (1.0 + gate * (1.0 - sigma))).astype(BF16),
            (hidden_grad * silu).astype(BF16),
        ],
        axis=1,
    )
    near_units, far_units = gather_over_row(units)
    def parts_by_core(blocks):
        blocks = lax.optimization_barrier(blocks)
        return [by_core([b[:, k * width : (k + 1) * width] for b in blocks]) for k in range(3)]

    near_units, far_units = parts_by_core(near_units), parts_by_core(far_units)

    def backward(units):
        hidden, gate_grad, up_grad = units
        grad = product_right_t(gate_grad, gate_weight) + product_right_t(up_grad, up_weight)
        return jnp.concatenate([product(hidden, down_weight), grad], axis=1)

    near_partial = backward(near_units)
    near_keep, _ = sum_over_core(near_partial, None)
    far_partial = backward(far_units)
    gain_partial = jnp.sum(near_partial[:, 1024:] * near_estimate, axis=0) + jnp.sum(
        far_partial[:, 1024:] * far_estimate, axis=0
    )
    far_keep, gain = sum_over_core(far_partial, gain_partial.reshape(8, 128))

    near_units, far_units, far_keep = lax.optimization_barrier((near_units, far_units, far_keep))

    def of_all(part):
        return jnp.concatenate([near_units[part], far_units[part]], axis=0)

    down_weight_grad = product_left_t(of_all(0), grad_full).astype(BF16)
    total, gain = sum_over_y(near_keep, far_keep, gain, x)
    normed, total, down_weight_grad = lax.optimization_barrier(
        (normed, total, down_weight_grad)
    )
    gate_weight_grad = product_left_t(normed, of_all(1)).astype(BF16)
    up_weight_grad = product_left_t(normed, of_all(2)).astype(BF16)

    gain_parts = [p.reshape(4, 256) for p in parts_of(gain, 2)]
    gain_rows = jnp.broadcast_to(jnp.concatenate(gain_parts, axis=1)[None], (16, 4, 512))
    total = total.astype(BF16)
    total = jnp.where(z == 0, total, jnp.concatenate([total[32:], total[:32]], axis=0))
    message = jnp.concatenate([total.reshape(16, 4, 2048), gain_rows], axis=2)
    back = lax.all_to_all(message, ("h", "z", "x"), split_axis=0, concat_axis=0, tiled=True)
    back = back.reshape(HS, 8, 4, 2560).astype(F32)
    gain_grad = back[..., 2048:2304] + back[..., 2304:]
    gain_grad = (gain_grad[0] + gain_grad[1]).reshape(8192)
    back = back[0, :, :, :2048] + back[1, :, :, :2048]
    outputs = jnp.transpose(back[..., :1024].astype(BF16), (1, 0, 2)).reshape(4, 8192)
    normed_grad = jnp.transpose(back[..., 1024:], (1, 0, 2)).reshape(4, 8192)

    normalized = value_entries * inverse_rms
    scaled = normed_grad * rms_gain_vector
    input_gradient = inverse_rms * (
        scaled - normalized * jnp.mean(scaled * normalized, axis=1, keepdims=True)
    )
    return (
        outputs,
        input_gradient.astype(BF16),
        gain_grad,
        gate_weight_grad,
        up_weight_grad,
        down_weight_grad,
    )


def solution(mesh):
    fine = Mesh(mesh.devices.reshape(ZS, XS, HS, YS, CS), AXES)
    row, col = AXES[:2], AXES[2:]
    in_specs = (P(AXES, None), P(), P(row, col), P(row, col), P(col, row), P(AXES, None))
    out_specs = (P(AXES, None), P(AXES, None), P(), P(row, col), P(row, col), P(col, row))
    return jax.shard_map(
        per_device, mesh=fine, in_specs=in_specs, out_specs=out_specs, check_vma=False
    )
```

```python
import jax
import jax.numpy as jnp
from jax import lax
from jax.sharding import Mesh, PartitionSpec as P

EPS = 1e-05
F32 = jnp.float32
BF16 = jnp.bfloat16
ZS, XS, HS, YS, CS = 2, 4, 2, 4, 2
AXES = ("z", "x", "h", "y", "core")


def send(value, z=0, x=0, h=0, y=0, c=0):
    pairs = []
    for z0 in range(ZS):
        for x0 in range(XS):
            for h0 in range(HS):
                for y0 in range(YS):
                    for c0 in range(CS):
                        source = (((z0 * XS + x0) * HS + h0) * YS + y0) * CS + c0
                        z1, x1, h1 = (z0 + z) % ZS, (x0 + x) % XS, (h0 + h) % HS
                        y1, c1 = (y0 + y) % YS, (c0 + c) % CS
                        pairs.append((source, (((z1 * XS + x1) * HS + h1) * YS + y1) * CS + c1))
    return lax.ppermute(value, AXES, pairs)


def product(left, right):
    return jnp.dot(left, right, preferred_element_type=F32)


def product_right_t(left, right):
    return lax.dot_general(left, right, (((1,), (1,)), ((), ())), preferred_element_type=F32)


def product_left_t(left, right):
    return lax.dot_general(left, right, (((0,), (0,)), ((), ())), preferred_element_type=F32)


def rounded(value):
    return lax.reduce_precision(value, 8, 7)


def parts_of(value, count):
    parts = []
    for _ in range(count):
        top = rounded(value)
        parts.append(top.astype(BF16))
        value = value - top
    return parts


def gather_half(own, x):
    n = own.shape[1]
    over_y = {0: own}
    for dy in (1, 3, 2):
        over_y[-dy % YS] = send(own, y=dy)
    core = jnp.zeros((128, n), own.dtype)
    for dy in range(YS):
        core = lax.dynamic_update_slice(core, over_y[dy], ((dy - x) % XS * 32, 0))
    return core, over_y[3]


def both_cores(core):
    return jnp.concatenate([core, send(core, c=1)], axis=0)


def by_core(blocks):
    return jnp.concatenate([b[:32] for b in blocks] + [b[32:] for b in blocks], axis=0)


def gain_of(parts):
    return parts[:8].astype(F32) + parts[8:16].astype(F32)


def sum_over_core(partial, gain_partial):
    give = partial[128:]
    if gain_partial is not None:
        give = give.astype(BF16)
        gain_rows = jnp.concatenate(parts_of(gain_partial, 2), axis=0)
        padded = jnp.pad(gain_rows, ((0, 0), (0, partial.shape[1] - 128)))
        give = jnp.concatenate([give, padded], axis=0)
    taken = send(give, c=1)
    if gain_partial is not None:
        gain_partial = gain_of(gain_rows) + gain_of(taken[128:, :128])
    return partial[:128] + taken[:128].astype(F32), gain_partial


def sum_over_y(near, far, gain, x):
    n = near.shape[1]

    def piece(dy):
        start = (dy - x) % XS * 32
        halves = [lax.dynamic_slice(half, (start, 0), (32, n)) for half in (near, far)]
        return jnp.concatenate(halves, axis=0)

    parts = jnp.concatenate(parts_of(gain, 2) + [jnp.zeros((48, 128), BF16)], axis=0)
    gains = {0: gain_of(parts)}
    total = piece(0)
    for dy in (1, 3, 2):
        got = send(jnp.concatenate([piece(dy).astype(BF16), parts], axis=1), y=dy)
        total = total + got[:, :n].astype(F32)
        gains[dy] = gain_of(got[:, n:])
    return total, (gains[0] + gains[2]) + (gains[1] + gains[3])


def sum_over_row(far, near):
    own, to1, to2, to3 = far
    near0, near1_top, near1_bottom, near2, near3_top, near3_bottom = near
    m12 = send(to2, z=1).astype(F32)
    m11 = send(to1, x=1).astype(F32)
    m13 = send(to3, x=3).astype(F32)
    first1 = send(near1_bottom, x=1)
    first2 = send(near3_top, x=3)
    n1 = send((near2[:32] + m12[:32]).astype(BF16), x=1).astype(F32)
    n2 = send((near2[32:] + m12[32:]).astype(BF16), x=3).astype(F32)
    q = send((own.astype(F32) + m11 + m13).astype(BF16), z=1)
    last1 = (near1_top + n1).astype(BF16)
    last2 = (near3_bottom + n2).astype(BF16)
    last1, last2, first1, first2 = lax.optimization_barrier((last1, last2, first1, first2))
    one = jnp.concatenate([send(last1, x=1), first1], axis=0).astype(F32)
    two = jnp.concatenate([first2, send(last2, x=3)], axis=0).astype(F32)
    return near0 + q.astype(F32) + one + two


def gather_over_row(own):
    h = own.shape[0] // 2
    a = send(own, x=1)
    b = send(own, x=3)
    p = send(own, z=1)
    a2 = send(a[:h], x=1)
    b2 = send(b[h:], x=3)
    pa = send(p, x=1)
    pb = send(p, x=3)
    across = jnp.concatenate([a2, b2], axis=0)
    p2 = send(across, z=1)
    return [own, b, across, a], [p, pb, p2, pa]


def per_device(inputs, rms_gain_vector, gate_weight, up_weight, down_weight, out_grad):
    z, x = lax.axis_index("z"), lax.axis_index("x")
    row = z * XS + x
    width = gate_weight.shape[1]

    value_entries = inputs.astype(F32)
    inverse_rms = lax.rsqrt(jnp.mean(value_entries * value_entries, axis=1, keepdims=True) + EPS)
    side = jnp.concatenate(parts_of(inverse_rms, 3) + [jnp.zeros((4, 125), BF16)], axis=1)
    message = jnp.concatenate(
        [
            inputs.reshape(4, 8, 1024),
            out_grad.reshape(4, 8, 1024),
            jnp.broadcast_to(side[:, None, :], (4, 8, 128)),
        ],
        axis=2,
    )
    message = jnp.broadcast_to(jnp.transpose(message, (1, 0, 2))[None], (HS, 8, 4, 2176))
    block = lax.all_to_all(
        message.reshape(16, 4, 2176), ("h", "z", "x"), split_axis=0, concat_axis=0, tiled=True
    )
    block = block.reshape(64, 2176)
    gain_block = lax.dynamic_slice(rms_gain_vector, (row * 1024,), (1024,))

    def normed_of(tokens):
        inverse = (
            tokens[:, 2048:2049].astype(F32)
            + tokens[:, 2049:2050].astype(F32)
            + tokens[:, 2050:2051].astype(F32)
        )
        estimate = tokens[:, :1024].astype(F32) * inverse
        return estimate, (estimate * gain_block).astype(BF16), tokens[:, 1024:2048]

    def partials(normed, grad):
        sums = [
            product(normed, gate_weight),
            product(normed, up_weight),
            product_right_t(grad, down_weight),
        ]

        def block(dx, dtype, cores=(0, 1)):
            rows = [
                jnp.concatenate([value[c * 128 + dx * 32 :][:32] for value in sums], axis=1)
                for c in cores
            ]
            return jnp.concatenate(rows, axis=0).astype(dtype)

        return block

    far_core, first = gather_half(lax.dynamic_slice(block, ((1 - z) * 32, 0), (32, 2176)), x)
    near_block, _ = lax.optimization_barrier(
        (lax.dynamic_slice(block, (z * 32, 0), (32, 2176)), first)
    )
    near_core, _ = gather_half(near_block, x)
    far_estimate, far_normed, far_grad = normed_of(both_cores(far_core))
    far = partials(far_normed, far_grad)
    far = [far(0, BF16), far(1, BF16), far(2, BF16), far(3, BF16)]
    near_core, far[0] = lax.optimization_barrier((near_core, far[0]))
    near_estimate, near_normed, near_grad = normed_of(both_cores(near_core))
    near = partials(near_normed, near_grad)
    near = [
        near(0, F32),
        near(1, F32, (0,)),
        near(1, BF16, (1,)),
        near(2, F32),
        near(3, BF16, (0,)),
        near(3, F32, (1,)),
    ]
    sums = sum_over_row(far, near)
    normed = jnp.concatenate([near_normed, far_normed], axis=0)
    grad_full = jnp.concatenate([near_grad, far_grad], axis=0)
    normed, grad_full, sums = lax.optimization_barrier((normed, grad_full, sums))
    gate, up, hidden_grad = sums[:, :width], sums[:, width : 2 * width], sums[:, 2 * width :]
    sigma = jax.nn.sigmoid(gate)
    silu = gate * sigma
    units = jnp.concatenate(
        [
            (silu * up).astype(BF16),
            (hidden_grad * up * sigma * (1.0 + gate * (1.0 - sigma))).astype(BF16),
            (hidden_grad * silu).astype(BF16),
        ],
        axis=1,
    )
    near_units, far_units = gather_over_row(units)
    def parts_by_core(blocks):
        blocks = lax.optimization_barrier(blocks)
        return [by_core([b[:, k * width : (k + 1) * width] for b in blocks]) for k in range(3)]

    near_units, far_units = parts_by_core(near_units), parts_by_core(far_units)

    def backward(units):
        hidden, gate_grad, up_grad = units
        grad = product_right_t(gate_grad, gate_weight) + product_right_t(up_grad, up_weight)
        return jnp.concatenate([product(hidden, down_weight), grad], axis=1)

    near_partial = backward(near_units)
    near_keep, _ = sum_over_core(near_partial, None)
    far_partial = backward(far_units)
    gain_partial = jnp.sum(near_partial[:, 1024:] * near_estimate, axis=0) + jnp.sum(
        far_partial[:, 1024:] * far_estimate, axis=0
    )
    far_keep, gain = sum_over_core(far_partial, gain_partial.reshape(8, 128))

    near_units, far_units, far_keep = lax.optimization_barrier((near_units, far_units, far_keep))

    def of_all(part):
        return jnp.concatenate([near_units[part], far_units[part]], axis=0)

    down_weight_grad = product_left_t(of_all(0), grad_full).astype(BF16)
    total, gain = sum_over_y(near_keep, far_keep, gain, x)
    normed, total, down_weight_grad = lax.optimization_barrier(
        (normed, total, down_weight_grad)
    )
    gate_weight_grad = product_left_t(normed, of_all(1)).astype(BF16)
    up_weight_grad = product_left_t(normed, of_all(2)).astype(BF16)

    gain_parts = [p.reshape(4, 256) for p in parts_of(gain, 2)]
    gain_rows = jnp.broadcast_to(jnp.concatenate(gain_parts, axis=1)[None], (16, 4, 512))
    total = total.astype(BF16)
    total = jnp.where(z == 0, total, jnp.concatenate([total[32:], total[:32]], axis=0))
    message = jnp.concatenate([total.reshape(16, 4, 2048), gain_rows], axis=2)
    back = lax.all_to_all(message, ("h", "z", "x"), split_axis=0, concat_axis=0, tiled=True)
    back = back.reshape(HS, 8, 4, 2560).astype(F32)
    gain_grad = back[..., 2048:2304] + back[..., 2304:]
    gain_grad = (gain_grad[0] + gain_grad[1]).reshape(8192)
    back = back[0, :, :, :2048] + back[1, :, :, :2048]
    outputs = jnp.transpose(back[..., :1024].astype(BF16), (1, 0, 2)).reshape(4, 8192)
    normed_grad = jnp.transpose(back[..., 1024:], (1, 0, 2)).reshape(4, 8192)

    normalized = value_entries * inverse_rms
    scaled = normed_grad * rms_gain_vector
    input_gradient = inverse_rms * (
        scaled - normalized * jnp.mean(scaled * normalized, axis=1, keepdims=True)
    )
    return (
        outputs,
        input_gradient.astype(BF16),
        gain_grad,
        gate_weight_grad,
        up_weight_grad,
        down_weight_grad,
    )


def solution(mesh):
    fine = Mesh(mesh.devices.reshape(ZS, XS, HS, YS, CS), AXES)
    row, col = AXES[:2], AXES[2:]
    in_specs = (P(AXES, None), P(), P(row, col), P(row, col), P(col, row), P(AXES, None))
    out_specs = (P(AXES, None), P(AXES, None), P(), P(row, col), P(row, col), P(col, row))
    return jax.shard_map(
        per_device, mesh=fine, in_specs=in_specs, out_specs=out_specs, check_vma=False
    )
```
